128 devices in a mesh: dp: 4 (over x), ch: 32 (over z, y, core).
Axes of the slice: x: 4, y: 4, z: 4, core: 2. Of those that a mesh axis runs over, the one named last changes fastest.
Arguments:
- block_input: bfloat16 [65536, 768], P(('dp', 'ch')), may hold values from -6 to 6
- gain_mix: float32 [768], replicated, may hold values from 0.25 to 1.75
- w_input: bfloat16 [768, 768], P(None, 'ch'), may hold values from -768 to 768
- w_forget: bfloat16 [768, 384], P(None, 'ch'), may hold values from -0.21875 to 0.21875
- w_outgate: bfloat16 [768, 768], P(None, 'ch'), may hold values from -0.21875 to 0.21875
- bias_forget: float32 [384], P('ch'), may hold values from -1 to 8192
- rotation: float32 [384], P('ch'), may hold values from -1 to 1
- w_out: bfloat16 [768, 768], P('ch'), may hold values from -0.4375 to 0.4375
- gain_mlp: float32 [768], replicated, may hold values from 0.25 to 1.75
- w_gate: bfloat16 [768, 1536], P(None, 'ch'), may hold values from -0.21875 to 0.21875
- w_up: bfloat16 [768, 1536], P(None, 'ch'), may hold values from -0.21875 to 0.21875
- w_down: bfloat16 [1536, 768], P('ch'), may hold values from -0.15625 to 0.15625
- seq_lengths: int32 [4, 8], P('dp'), may hold values from 1 to 8192, as said below
- pad_mask: int32 [65536], P(('dp', 'ch')), may hold values from 0 to 1, as said below
- cotangent: bfloat16 [65536, 768], P(('dp', 'ch')), may hold values from -6 to 6
Outputs:
- block_output: bfloat16 [65536, 768], P(('dp', 'ch'))
- grad_input: bfloat16 [65536, 768], P(('dp', 'ch'))
- grad_gain_mix: float32 [768], replicated
- grad_w_input: float32 [768, 768], P(None, 'ch')
- grad_w_forget: float32 [768, 384], P(None, 'ch')
- grad_w_outgate: float32 [768, 768], P(None, 'ch')
- grad_bias_forget: float32 [384], P('ch')
- grad_rotation: float32 [384], P('ch')
- grad_w_out: float32 [768, 768], P('ch')
- grad_gain_mlp: float32 [768], replicated
- grad_w_gate: float32 [768, 1536], P(None, 'ch')
- grad_w_up: float32 [768, 1536], P(None, 'ch')
- grad_w_down: float32 [1536, 768], P('ch')
The draws below stay inside these ranges and needn't reach their ends.
Inputs may be any that keep to these rules, and one draw needn't show every extreme that they name: `seq_lengths`: each row lists the lengths of the 8 sequences laid end to end over one group's 16384 rows; they sum to 16384, and exactly one in each row equals 8192. `pad_mask`: 0 stands only in a tail of a sequence, at most a quarter of its length rounded down.
All inputs are finite; a program needn't handle non-finite values.
Results may differ from the reference program's by a relative error of at most 0.017.
Values may be sent and summed in bfloat16 or wider, within the bound.
No kernel may reach another device: no remote copies, remote signals or barrier semaphores. Data moves between devices by JAX's collectives and lax.ppermute only.
A program may use at most 448 MiB of HBM per device.

```python
import math
import jax
import jax.numpy as jnp
from jax import lax

D = 768
CH = 384
FF = 1536
SEQS = 8
GROUP_TOK = 16384
MOST = 8192
TOKENS = 65536
N_DP = 4


def sequence_lengths(key):
    remaining = GROUP_TOK - MOST

    def one_row(row_key):
        key_cut = jax.random.fold_in(row_key, 1)
        key_slot = jax.random.fold_in(row_key, 2)
        cut_points = jnp.sort(jax.random.permutation(key_cut, remaining - 1)[:SEQS - 2] + 1).astype(jnp.int32)
        boundaries = jnp.concatenate([jnp.zeros((1,), jnp.int32), cut_points, jnp.full((1,), remaining, jnp.int32)])
        others = boundaries[1:] - boundaries[:-1]
        lengths_row = jnp.concatenate([jnp.full((1,), MOST, jnp.int32), others])
        return jnp.roll(lengths_row, jax.random.randint(key_slot, (), 0, SEQS))
    return jax.vmap(one_row)(jax.random.split(key, N_DP))


def lasting_channels(key, portion):
    picks = jax.random.uniform(jax.random.fold_in(key, 101), (CH,), jnp.float32)
    return (picks < portion).astype(jnp.float32)


def draw_seq_lengths(key, part):
    return sequence_lengths(key)


def draw_pad_mask(key, part):
    lengths_all = sequence_lengths(key)
    key = jax.random.fold_in(key, 7)
    pad_counts = jax.random.randint(key, lengths_all.shape, 0, 1 << 20) % (lengths_all // 4 + 1)
    end_pos = jnp.cumsum(lengths_all, axis=1)
    positions = jnp.arange(GROUP_TOK, dtype=jnp.int32)[None, :, None]
    padded = (positions >= (end_pos - pad_counts)[:, None, :]) & (positions < end_pos[:, None, :])
    return (1 - jnp.any(padded, axis=2).astype(jnp.int32)).reshape(TOKENS)


def draw_bias_forget(key, part):
    portion = 0.5
    lasting = lasting_channels(key, portion)
    key = jax.random.fold_in(key, 11)
    quick_bias = jax.random.uniform(jax.random.fold_in(key, 1), (CH,), jnp.float32, -1.0, 3.0)
    slow_bias = jax.random.uniform(jax.random.fold_in(key, 2), (CH,), jnp.float32, math.log(0.6 * MOST), math.log(2.5 * MOST))
    return lasting * slow_bias + (1.0 - lasting) * quick_bias


def draw_rotation(key, part):
    portion = 0.5
    factor = 2.0
    lasting = lasting_channels(key, portion)
    key = jax.random.fold_in(key, 12)
    turns = jax.random.uniform(key, (CH,), jnp.float32, -0.4, 0.4)
    return turns * (lasting * (factor / MOST) + (1.0 - lasting))


def draw_w_input(key, part):
    key = jax.random.fold_in(key, 13)
    factor = 1.0
    return (jax.random.normal(key, (D, 2 * CH), jnp.float32) * (factor / math.sqrt(D))).astype(jnp.bfloat16)


def levels(stream_key, dims, shards, least, largest):
    loudness, own = 1.0, jax.random.fold_in(stream_key, 6)
    for dim, blocks in shards:
        steps = jnp.exp(jax.random.uniform(jax.random.fold_in(own, dim), (blocks,), jnp.float32, least / len(shards), largest / len(shards)))
        loudness = loudness * jnp.repeat(steps, dims[dim] // blocks).reshape([-1 if axis == dim else 1 for axis in range(len(dims))])
    return loudness


def gaussian(key, shape, deviation, bound, pieces=(), held_as=jnp.bfloat16):
    array = deviation * jax.random.normal(key, shape, jnp.float32)
    if pieces:
        array = array * levels(key, shape, pieces, -0.22, 0.18)
    return jnp.clip(array, -bound, bound).astype(held_as)


def setup_inputs(seed: int = 0) -> dict:
    splits = jax.random.split(jax.random.key(seed), 16)
    return {
        "block_input": gaussian(splits[0], (TOKENS, D), 1.0, 6.0, ((0, 128),)),
        "gain_mix": jnp.clip(1.0 + 0.15 * jax.random.normal(splits[1], (D,), jnp.float32), 0.25, 1.75),
        "w_input": draw_w_input(jax.random.fold_in(splits[15], 71), 0),
        "w_forget": gaussian(splits[3], (D, CH), D ** -0.5, 0.21875, ((1, 32),)),
        "w_outgate": gaussian(splits[4], (D, 2 * CH), D ** -0.5, 0.21875, ((1, 32),)),
        "bias_forget": draw_bias_forget(jax.random.fold_in(splits[15], 71), 0),
        "rotation": draw_rotation(jax.random.fold_in(splits[15], 71), 0),
        "w_out": gaussian(splits[7], (2 * CH, D), (CH // 2) ** -0.5, 0.4375, ((0, 32),)),
        "gain_mlp": jnp.clip(1.0 + 0.15 * jax.random.normal(splits[8], (D,), jnp.float32), 0.25, 1.75),
        "w_gate": gaussian(splits[9], (D, FF), D ** -0.5, 0.21875, ((1, 32),)),
        "w_up": gaussian(splits[10], (D, FF), D ** -0.5, 0.21875, ((1, 32),)),
        "w_down": gaussian(splits[11], (FF, D), FF ** -0.5, 0.15625, ((0, 32),)),
        "seq_lengths": draw_seq_lengths(jax.random.fold_in(splits[15], 71), 0),
        "pad_mask": draw_pad_mask(jax.random.fold_in(splits[15], 71), 0),
        "cotangent": gaussian(splits[14], (TOKENS, D), 1.0, 6.0, ((0, 128),)),
    }


EPSILON = 1e-06

@jax.custom_vjp
def low(v):
    return lax.optimization_barrier(v.astype(jnp.bfloat16)).astype(jnp.float32)

@jax.custom_vjp
def low_back(v):
    return v

def low_keep(v):
    return (low(v), None)

def low_pass(kept, grad):
    return (grad,)

def back_keep(v):
    return (v, None)

def back_low(kept, grad):
    return (low(grad),)
low.defvjp(low_keep, low_pass)
low_back.defvjp(back_keep, back_low)

def product(left_op, right_op):
    return jnp.dot(left_op, right_op, precision=lax.Precision.HIGHEST, preferred_element_type=jnp.float32)

def rms_scaled(values, gain):
    return values * lax.rsqrt(lax.optimization_barrier(jnp.mean(values * values, axis=-1, keepdims=True)) + EPSILON) * gain

def start_flags(seq_lengths):
    end_pos = jnp.cumsum(seq_lengths, axis=1).astype(jnp.int32)
    starts = (end_pos - seq_lengths).astype(jnp.int32)
    positions = jnp.arange(GROUP_TOK, dtype=jnp.int32)
    matches = positions[None, :, None] == starts[:, None, :]
    return jnp.any(matches, axis=2).astype(jnp.float32).reshape(TOKENS)

def recurrence(mult_re, mult_im, add_re, add_im):
    block_len = math.gcd(GROUP_TOK, 64)

    def to_time(stacked):
        return stacked.reshape(N_DP, GROUP_TOK // block_len, block_len, CH).transpose(1, 2, 0, 3)

    def from_time(stacked):
        return stacked.transpose(2, 0, 1, 3).reshape(TOKENS, CH)

    def one_step(carried, inputs):
        state_re, state_im = carried
        step_mre, step_mim, step_are, step_aim = inputs
        new_re = step_mre * state_re - step_mim * state_im + step_are
        new_im = step_mre * state_im + step_mim * state_re + step_aim
        return ((new_re, new_im), (new_re, new_im))

    @jax.checkpoint
    def one_block(carried, inputs):
        return lax.scan(one_step, carried, inputs)
    initial = (jnp.zeros((N_DP, CH), jnp.float32), jnp.zeros((N_DP, CH), jnp.float32))
    streams = tuple((to_time(stacked) for stacked in (mult_re, mult_im, add_re, add_im)))
    final_state, outputs = lax.scan(one_block, initial, streams)
    return (from_time(outputs[0]), from_time(outputs[1]))

def block_forward(block_input, gain_mix, w_input, w_forget, w_outgate, bias_forget, rotation, w_out, gain_mlp, w_gate, w_up, w_down, keep_rows, first_rows):
    normed = low(rms_scaled(block_input, gain_mix) * keep_rows[:, None])
    pre_in = low_back(product(normed, w_input))
    pre_forget = low_back(product(normed, w_forget))
    pre_gate = low_back(product(normed, w_outgate))
    values = jax.nn.silu(pre_in).reshape(TOKENS, CH, 2)
    decay_rate = jax.nn.sigmoid(pre_forget + bias_forget)
    retain = decay_rate * (1.0 - first_rows)[:, None]
    admitted = 1.0 - decay_rate
    states_re, states_im = recurrence(retain * jnp.cos(rotation), retain * jnp.sin(rotation), admitted * values[:, :, 0], admitted * values[:, :, 1])
    hidden = jnp.stack([states_re, states_im], axis=-1).reshape(TOKENS, 2 * CH)
    gated_out = low(hidden * jax.nn.sigmoid(pre_gate))
    mixed_rows = block_input + low_back(product(gated_out, w_out))
    normed_mlp = low(rms_scaled(mixed_rows, gain_mlp))
    gate_pre = low_back(product(normed_mlp, w_gate))
    up_pre = low_back(product(normed_mlp, w_up))
    activated = low(jax.nn.silu(gate_pre) * up_pre)
    return mixed_rows + low_back(product(activated, w_down))

def reference(block_input, gain_mix, w_input, w_forget, w_outgate, bias_forget, rotation, w_out, gain_mlp, w_gate, w_up, w_down, seq_lengths, pad_mask, cotangent):
    keep_rows = pad_mask.astype(jnp.float32)
    first_rows = start_flags(seq_lengths)

    def closed(*operands):
        return block_forward(*operands, keep_rows, first_rows)
    operands = (block_input.astype(jnp.float32), gain_mix, w_input.astype(jnp.float32), w_forget.astype(jnp.float32), w_outgate.astype(jnp.float32), bias_forget, rotation, w_out.astype(jnp.float32), gain_mlp, w_gate.astype(jnp.float32), w_up.astype(jnp.float32), w_down.astype(jnp.float32))
    output, pullback = jax.vjp(closed, *operands)
    gradients = pullback(cotangent.astype(jnp.float32) * keep_rows[:, None])
    return (output.astype(jnp.bfloat16), gradients[0].astype(jnp.bfloat16), gradients[1], gradients[2], gradients[3], gradients[4], gradients[5], gradients[6], gradients[7], gradients[8], gradients[9], gradients[10], gradients[11])
```

```python
import jax
import jax.numpy as jnp
from jax import lax
from jax.experimental import pallas as pl
from jax.experimental.pallas import tpu as pltpu
from jax.sharding import PartitionSpec as P

EPS = 1e-06
F32 = jnp.float32
BF16 = jnp.bfloat16

ROWS = 512
D = 768
H = 384
CH = 384
FF = 1536
SEG = 8
STEPS = ROWS // SEG
NZ, NY, NX = 4, 4, 4
UNIT = 24
MIX_U = 7
VEC = 96 * MIX_U
COS, SIN, C64, S64, C512, S512, BIAS = 0, 64, 128, 129, 130, 131, 132
TAB = 136
SWAP = (0, 2, 1, 3)


def nt(a, b):
    return lax.dot_general(a, b, (((1,), (1,)), ((), ())), preferred_element_type=F32)


def nn(a, b):
    return lax.dot_general(a, b, (((1,), (0,)), ((), ())), preferred_element_type=F32)


def tn(a, b):
    return lax.dot_general(a, b, (((0,), (0,)), ((), ())), preferred_element_type=F32)


def exact(a, b):
    return lax.dot_general(
        a, b, (((1,), (0,)), ((), ())), precision=lax.Precision.HIGHEST, preferred_element_type=F32
    )


def exact_t(a, b):
    return lax.dot_general(
        a, b, (((1,), (1,)), ((), ())), precision=lax.Precision.HIGHEST, preferred_element_type=F32
    )


def wide(col):
    return jnp.concatenate([col, col, col], axis=1)


def loop(count, size, body, start=0):
    def step(i, _):
        body(pl.ds(pl.multiple_of(i * size, size), size), i)
        return 0

    lax.fori_loop(start, count, step, 0)


class Copies:
    def __init__(self, sems):
        self.sems = sems
        self.used = 0
        self.open = {}

    def __call__(self, name, src, dst):
        copy = pltpu.make_async_copy(src, dst, self.sems.at[self.used])
        self.used += 1
        copy.start()
        self.open.setdefault(name, []).append(copy)

    def wait(self, *names):
        for name in names:
            for copy in self.open.pop(name):
                copy.wait()

    def finish(self):
        self.wait(*list(self.open))


def fetch_mix(cp, name, pieces, units, scratch, at):
    for u in range(units[0], units[0] + units[1]):
        for half in range(2):
            for k in range(4):
                cp(
                    name,
                    pieces[half * 4 + (SWAP[k] if half else k)].at[pl.ds(96 * u, 96)],
                    scratch.at[at + u - units[0], pl.ds(96 * k, 96), pl.ds(H * half, H)],
                )


def fetch_mlp(cp, name, pieces, kind, scratch):
    for half in range(2):
        for k in range(4):
            cp(
                name,
                pieces[half * 4 + (SWAP[k] if half else k)].at[kind],
                scratch.at[kind, pl.ds(CH * k, CH), pl.ds(H * half, H)],
            )


def put_grad(grad, unit, mine, other):
    low = grad.astype(BF16)
    for k in range(4):
        mine[k, unit] = low[96 * k : 96 * k + 96, :H]
        other[SWAP[k], unit] = low[96 * k : 96 * k + 96, H:]


def turns(tab, i, steps):
    rows = []
    for base in (COS, SIN):
        parts = [
            jnp.broadcast_to(tab[pl.ds(base + i * steps + s, 1), :], (SEG, CH)) for s in range(steps)
        ]
        rows.append(parts[0] if steps == 1 else jnp.concatenate(parts, axis=0))
    return rows


def row(ref, i):
    return ref[i : i + 1, :]


def summaries(cp, me, pieces, order):
    core = me[0] % 2
    y = (me[0] // 2) % NY
    z = me[0] // (2 * NY)
    for kz in range(NZ):
        for ky in range(NY):
            for kc in range(2):
                place = (((z + kz) % NZ) * NY + (y + ky) % NY) * 2 + (core + kc) % 2
                cp(
                    "order",
                    pieces[ky].at[pl.ds((kz * 2 + kc) * SEG, SEG)],
                    order.at[pl.ds(pl.multiple_of(place * SEG, SEG), SEG)],
                )


def k_norm(x_h, keep_h, gain_h, normed_h, x, keep, gain, normed, sems):
    cp = Copies(sems)
    cp("x", x_h, x)
    cp("x", keep_h, keep)
    cp("x", gain_h, gain)
    cp.wait("x")

    def norm(r, i):
        v = x[r, :].astype(F32)
        rs = lax.rsqrt(jnp.mean(v * v, axis=-1, keepdims=True) + EPS) * keep[r, :1]
        normed[r, :] = (v * rs * gain[...]).astype(BF16)

    loop(8, 64, norm)
    cp("out", normed, normed_h)
    cp.finish()


def k_project(me, normed_h, nf_h, perm_h, *rest):
    pieces = rest[:8]
    pre_h, s_h, lam_h, cum_h, tab_h, summary_h = rest[8:14]
    w, normed, nf, perm, vecs, pre, pf, s, lam, cum, tab, sums, sems = rest[14:]
    cp = Copies(sems)
    for i in range(8):
        cp("vecs", pieces[i].at[pl.ds(VEC, 32)], vecs.at[pl.ds(32 * i, 32)])
    cp("w", normed_h, normed)
    fetch_mix(cp, "w", pieces, (0, 3), w, 0)
    cp("nf", perm_h, perm)
    cp("nf", nf_h, nf)

    cp.wait("vecs")
    group = lax.broadcasted_iota(jnp.int32, (32, 256), 0)
    half = (group + me[0]) % 2
    kz = group // 8
    kz = jnp.where((half == 1) & (kz > 0) & (kz < 3), 3 - kz, kz)
    source = 32 * (half * 4 + kz) + 8 * ((group // 2) % 4)
    choose = jnp.where(source == lax.broadcasted_iota(jnp.int32, (32, 256), 1), 1.0, 0.0).astype(BF16)
    values = nn(choose, vecs[...])[:, :128].astype(BF16)
    sub = lax.broadcasted_iota(jnp.int32, (128, CH), 0)
    same = (sub % 12 == lax.broadcasted_iota(jnp.int32, (128, CH), 1) % 12) & (sub < 72)
    hit = lax.broadcasted_iota(jnp.int32, (32, CH), 0) == lax.broadcasted_iota(jnp.int32, (32, CH), 1) // 12
    found = []
    for v in range(2):
        pick = jnp.where(same & ((sub % 24) // 12 == v), 1.0, 0.0).astype(BF16)
        found.append(jnp.sum(jnp.where(hit, nn(values, pick), 0.0), axis=0, keepdims=True))
    bias, rot = found
    few = lax.broadcasted_iota(jnp.int32, (SEG, CH), 0)
    one = few.astype(F32) * rot
    eight = one * 8.0
    far = jnp.where(few < 2, float(STEPS), float(ROWS)) * rot
    c_one, s_one, c_eight, s_eight = jnp.cos(one), jnp.sin(one), jnp.cos(eight), jnp.sin(eight)
    for i in range(SEG):
        ca, sa = c_eight[i : i + 1], s_eight[i : i + 1]
        tab[COS + SEG * i : COS + SEG * i + SEG, :] = ca * c_one - sa * s_one
        tab[SIN + SEG * i : SIN + SEG * i + SEG, :] = sa * c_one + ca * s_one
    cos, sin = jnp.cos(far), jnp.sin(far)
    c64, s64 = cos[0:1], sin[0:1]
    cp.wait("nf")
    far = exact(jnp.where(few % 2 == 0, cos, sin), perm[...])
    tab[C64:TAB, :] = jnp.zeros((SEG, CH), F32)
    tab[C64 : C64 + 1, :] = c64
    tab[S64 : S64 + 1, :] = s64
    tab[C512 : C512 + 1, :] = far[2:3]
    tab[S512 : S512 + 1, :] = far[3:4]
    cp("out", tab, tab_h)

    cp.wait("w")
    n = normed[...]
    pre[:, 0:CH] = nt(n, w[0])
    pre[:, CH:] = nt(n, w[1])
    pf[...] = nt(n, w[2])
    cp("out", pre, pre_h)

    def step(t, carry):
        sr, si, p = carry
        r = pl.ds(pl.multiple_of(t * SEG, SEG), SEG)
        l = jax.nn.sigmoid(pf[r, :] + bias)
        a = l * wide(nf[r, :])
        adm = 1.0 - l
        vr = pre[r, 0:CH]
        vi = pre[r, CH:]
        vr = adm * vr * jax.nn.sigmoid(vr)
        vi = adm * vi * jax.nn.sigmoid(vi)
        ct, st = turns(tab, t, 1)
        sr = a * sr + (vr * ct + vi * st)
        si = a * si + (vi * ct - vr * st)
        p = a * p
        lam[r, :] = l
        s[r, 0:CH] = sr
        s[r, CH:] = si
        cum[r, :] = p
        return sr, si, p

    zero = jnp.zeros((SEG, CH), F32)
    sr, si, p = lax.fori_loop(0, STEPS, step, (zero, zero, zero + 1.0), unroll=4)
    cp("out", s, s_h)
    cp("out", lam, lam_h)
    cp("out", cum, cum_h)
    er = jnp.zeros((1, CH), F32)
    ei = jnp.zeros((1, CH), F32)
    pt = jnp.ones((1, CH), F32)
    for b in range(SEG):
        pb = p[b : b + 1]
        tr = sr[b : b + 1] + pb * er
        ti = si[b : b + 1] + pb * ei
        er = c64 * tr - s64 * ti
        ei = c64 * ti + s64 * tr
        pt = pt * pb
    sums[...] = jnp.zeros_like(sums)
    sums[0:1, :] = pt
    sums[1:2, :] = er
    sums[2:3, :] = ei
    sums[...] = exact(sums[...], perm[...])
    cp("out", sums, summary_h)
    cp.finish()


def k_gate(normed_h, *rest):
    pieces = rest[:8]
    pg_h, w, normed, pg, sems = rest[8:]
    cp = Copies(sems)
    cp("w", normed_h, normed)
    fetch_mix(cp, "w", pieces, (3, 2), w, 0)
    cp.wait("w")
    pg[...] = nt(normed[...], w[...].reshape(2 * CH, D))
    cp("out", pg, pg_h)
    cp.finish()


def k_ffn(me, gat0, gat1, gat2, gat3, tab_h, perm_h, s_h, cum_h, pg_h, x_h, gain_h, ups_h, *rest):
    mix_p, mlp_p = rest[:8], rest[8:16]
    t_h, sg_h, gated_h, mixed_h, enter_h, out_h, bmlp_h, mine_h, other_h = rest[16:25]
    (wo, w, order, tab, perm, s, cum, pg, x, gain, ups, sums, enter, gated, mixed, nm, act, bg, bu, out, bmlp,
     mine, other, sems) = rest[25:]
    cp = Copies(sems)
    summaries(cp, me, (gat0, gat1, gat2, gat3), order)
    cp("order", tab_h, tab)
    cp("order", perm_h, perm)
    cp("s", s_h, s)
    cp("s", cum_h, cum)
    cp("s", pg_h, pg)
    fetch_mix(cp, "wo", mix_p, (5, 2), wo, 0)
    cp("x", x_h, x)
    cp("x", gain_h, gain)
    for kind in range(3):
        fetch_mlp(cp, ("gate", "up", "down")[kind], mlp_p, kind, w)
    cp("ups", ups_h, ups)

    cp.wait("order")
    c512, s512 = row(tab, C512), row(tab, S512)
    c64, s64 = row(tab, C64), row(tab, S64)
    er = jnp.zeros((1, CH), F32)
    ei = jnp.zeros((1, CH), F32)
    for d in range(31):
        pd = row(order, 8 * d)
        nr = row(order, 8 * d + 1) + pd * (c512 * er - s512 * ei)
        ni = row(order, 8 * d + 2) + pd * (c512 * ei + s512 * er)
        er = jnp.where(d < me[0], nr, er)
        ei = jnp.where(d < me[0], ni, ei)
    sums[...] = jnp.zeros_like(sums)
    sums[0:1, :] = er
    sums[1:2, :] = ei
    back = exact_t(sums[...], perm[...])
    er = back[0:1, :]
    ei = back[1:2, :]
    cp.wait("s")
    last = ROWS - SEG
    for b in range(SEG):
        enter[b : b + 1, :] = er
        enter[SEG + b : SEG + b + 1, :] = ei
        pb = row(cum, last + b)
        tr = s[last + b : last + b + 1, 0:CH] + pb * er
        ti = s[last + b : last + b + 1, CH:] + pb * ei
        er = c64 * tr - s64 * ti
        ei = c64 * ti + s64 * tr
    cp("out", enter, enter_h)

    def fix(r, i):
        ber = enter[0:SEG, :]
        bei = enter[SEG : 2 * SEG, :]
        ber = jnp.concatenate([ber, ber], axis=0)
        bei = jnp.concatenate([bei, bei], axis=0)
        p = cum[r, :]
        sr = s[r, 0:CH] + p * ber
        si = s[r, CH:] + p * bei
        s[r, 0:CH] = sr
        s[r, CH:] = si
        ct, st = turns(tab, i, 2)
        gr = jax.nn.sigmoid(pg[r, 0:CH])
        gi = jax.nn.sigmoid(pg[r, CH:])
        pg[r, 0:CH] = gr
        pg[r, CH:] = gi
        gated[r, 0:CH] = ((sr * ct - si * st) * gr).astype(BF16)
        gated[r, CH:] = ((sr * st + si * ct) * gi).astype(BF16)

    loop(32, 16, fix)
    cp("out", s, t_h)
    cp("out", pg, sg_h)
    cp("out", gated, gated_h)
    cp.wait("wo")
    mixed[...] = nn(gated[...], wo[...].reshape(2 * CH, D))
    cp.wait("x")

    def norm(r, i):
        v = mixed[r, :] + x[r, :].astype(F32)
        mixed[r, :] = v
        rs = lax.rsqrt(jnp.mean(v * v, axis=-1, keepdims=True) + EPS)
        nm[r, :] = (v * rs * gain[...]).astype(BF16)

    loop(8, 64, norm)
    cp("out", mixed, mixed_h)
    n = nm[...]
    cp.wait("gate", "up", "down", "ups")
    up_low = ups[...]
    for k in range(4):
        cols = slice(CH * k, CH * k + CH)
        gp = nt(n, w[0, cols, :])
        up = nt(n, w[1, cols, :])
        ba = nt(up_low, w[2, cols, :])
        sg = jax.nn.sigmoid(gp)
        ga = gp * sg
        act[:, cols] = (ga * up).astype(BF16)
        bg[:, cols] = (ba * up * sg * (1.0 + gp * (1.0 - sg))).astype(BF16)
        bu[:, cols] = (ba * ga).astype(BF16)
    for kind, (left, right) in enumerate(((bg, n), (bu, n), (act, up_low))):
        for k in range(4):
            grad = tn(left[:, CH * k : CH * k + CH], right)
            for j in range(4):
                part = jnp.concatenate(
                    [grad[96 * i + UNIT * j : 96 * i + UNIT * j + UNIT] for i in range(4)], axis=0
                ).astype(BF16)
                mine[kind * 4 + j, 96 * k : 96 * k + 96, :] = part[:, :H]
                other[kind * 4 + j, 96 * SWAP[k] : 96 * SWAP[k] + 96, :] = part[:, H:]
        for j in range(4):
            unit = kind * 4 + j
            cp("out", other.at[unit], other_h.at[me[6 + unit // 3], unit % 3])
            cp("out", mine.at[unit], mine_h.at[me[2 + unit // 3], unit % 3])
    bmlp[...] = nn(bg[...], w[0]) + nn(bu[...], w[1])
    cp("out", bmlp, bmlp_h)
    out[...] = (mixed[...] + nn(act[...], w[2])).astype(BF16)
    cp("out", out, out_h)
    cp.finish()


def k_back(me, bmlp_h, mixed_h, ups_h, gain_h, sg_h, lam_h, nf_h, tab_h, perm_h, *rest):
    mix_p = rest[:8]
    bm_h, gpart_h, bgt_h, g_h, q_h, summary_h, bml_h = rest[8:15]
    wo, bmlp, mixed, ups, gain, sg, lam, nf, tab, perm, bm, bgt, g, q, bml, sums, gsum, sems = rest[15:]
    cp = Copies(sems)
    cp("a", bmlp_h, bmlp)
    cp("a", mixed_h, mixed)
    cp("a", ups_h, ups)
    cp("a", gain_h, gain)
    fetch_mix(cp, "wo", mix_p, (5, 2), wo, 0)
    cp("b", sg_h, sg)
    cp("b", lam_h, lam)
    cp("b", nf_h, nf)
    cp("b", tab_h, tab)
    cp("perm", perm_h, perm)
    gsum[...] = jnp.zeros_like(gsum)
    cp.wait("a")

    def norm(r, i):
        v = mixed[r, :]
        b = bmlp[r, :]
        rs = lax.rsqrt(jnp.mean(v * v, axis=-1, keepdims=True) + EPS)
        gsum[...] += jnp.sum(b * v * rs, axis=0, keepdims=True)
        u2 = b * gain[...]
        m = jnp.mean(u2 * v, axis=-1, keepdims=True)
        o = ups[r, :].astype(F32) + rs * u2 - v * (rs * rs * rs * m)
        bm[r, :] = o
        bml[r, :] = o.astype(BF16)

    loop(8, 64, norm)
    cp("out", bm, bm_h)
    cp("out", bml, bml_h)
    cp("out", gsum, gpart_h)
    cp.wait("wo")
    bgt[...] = nt(bml[...], wo[...].reshape(2 * CH, D))
    cp("out", bgt, bgt_h)
    cp.wait("b")
    c64, s64 = row(tab, C64), row(tab, S64)

    def step(i, carry):
        cr, ci, p = carry
        t = STEPS - 1 - i
        r = pl.ds(pl.multiple_of(t * SEG, SEG), SEG)
        gr = bgt[r, 0:CH] * sg[r, 0:CH]
        gi = bgt[r, CH:] * sg[r, CH:]
        ct, st = turns(tab, t, 1)
        a = lam[r, :] * wide(nf[r, :])
        gr, gi = gr * ct + gi * st + cr, gi * ct - gr * st + ci
        g[r, 0:CH] = gr
        g[r, CH:] = gi
        q[r, :] = p
        return a * gr, a * gi, a * p

    zero = jnp.zeros((SEG, CH), F32)
    cr, ci, p = lax.fori_loop(0, STEPS, step, (zero, zero, zero + 1.0), unroll=4)
    er = jnp.zeros((1, CH), F32)
    ei = jnp.zeros((1, CH), F32)
    pt = jnp.ones((1, CH), F32)
    for b in range(SEG - 1, -1, -1):
        pb = p[b : b + 1, :]
        tr = cr[b : b + 1, :] + pb * er
        ti = ci[b : b + 1, :] + pb * ei
        er = c64 * tr + s64 * ti
        ei = c64 * ti - s64 * tr
        pt = pt * pb
    sums[...] = jnp.zeros_like(sums)
    sums[0:1, :] = pt
    sums[1:2, :] = er
    sums[2:3, :] = ei
    cp.wait("perm")
    sums[...] = exact(sums[...], perm[...])
    cp("out", sums, summary_h)
    cp("out", g, g_h)
    cp("out", q, q_h)
    cp.finish()


def k_mid(bgt_h, t_h, sg_h, tab_h, normed_h, gated_h, bml_h, *rest):
    bpg_h, mine_h, other_h = rest[:3]
    bgt, t, sg, tab, normed, gated, bml, bpg, mine, other, sems = rest[3:]
    cp = Copies(sems)
    cp("b", gated_h, gated)
    cp("b", bml_h, bml)
    cp("a", bgt_h, bgt)
    cp("a", t_h, t)
    cp("a", sg_h, sg)
    cp("a", tab_h, tab)
    cp("c", normed_h, normed)
    cp.wait("b")
    b = bml[...]
    put_grad(tn(gated[:, 0:CH], b), 2, mine, other)
    put_grad(tn(gated[:, CH:], b), 3, mine, other)
    cp.wait("a")

    def gate(r, i):
        sr = t[r, 0:CH]
        si = t[r, CH:]
        ct, st = turns(tab, i, 2)
        gr = sg[r, 0:CH]
        gi = sg[r, CH:]
        bpg[r, 0:CH] = (bgt[r, 0:CH] * (sr * ct - si * st) * gr * (1.0 - gr)).astype(BF16)
        bpg[r, CH:] = (bgt[r, CH:] * (sr * st + si * ct) * gi * (1.0 - gi)).astype(BF16)

    loop(32, 16, gate)
    cp("out", bpg, bpg_h)
    cp.wait("c")
    n = normed[...]
    put_grad(tn(bpg[:, 0:CH], n), 0, mine, other)
    put_grad(tn(bpg[:, CH:], n), 1, mine, other)
    cp("out", other, other_h)
    cp("out", mine, mine_h)
    cp.finish()


def k_last(me, gat0, gat1, gat2, gat3, tab_h, perm_h, g_h, q_h, lam_h, nf_h, t_h, enter_h, pre_h, normed_h, *rest):
    bpi_h, bpf_h, parts_h, mine_h, other_h = rest[:5]
    order, tab, perm, g, q, lam, nf, t, enter, pre, normed, bpi, bpf, mine, other, lead, sums, sems = rest[5:]
    cp = Copies(sems)
    summaries(cp, me, (gat0, gat1, gat2, gat3), order)
    cp("order", tab_h, tab)
    cp("order", perm_h, perm)
    cp("a", g_h, g)
    cp("a", q_h, q)
    cp("a", lam_h, lam)
    cp("a", nf_h, nf)
    cp("a", t_h, t)
    cp("a", enter_h, enter)
    cp("a", pre_h, pre)
    cp("b", normed_h, normed)
    cp.wait("order")
    c512, s512 = row(tab, C512), row(tab, S512)
    c64, s64 = row(tab, C64), row(tab, S64)
    er = jnp.zeros((1, CH), F32)
    ei = jnp.zeros((1, CH), F32)
    for d in range(31, 0, -1):
        pd = row(order, 8 * d)
        nr = row(order, 8 * d + 1) + pd * (c512 * er + s512 * ei)
        ni = row(order, 8 * d + 2) + pd * (c512 * ei - s512 * er)
        er = jnp.where(d > me[0], nr, er)
        ei = jnp.where(d > me[0], ni, ei)
    sums[...] = jnp.zeros_like(sums)
    sums[0:1, :] = er
    sums[1:2, :] = ei
    back = exact_t(sums[0:SEG, :], perm[...])
    er = back[0:1, :]
    ei = back[1:2, :]
    cp.wait("a")
    for b in range(SEG - 1, -1, -1):
        lead[b : b + 1, :] = er
        lead[SEG + b : SEG + b + 1, :] = ei
        a0 = row(lam, b) * wide(row(nf, b))
        tr = a0 * (g[b : b + 1, 0:CH] + row(q, b) * er)
        ti = a0 * (g[b : b + 1, CH:] + row(q, b) * ei)
        er = c64 * tr + s64 * ti
        ei = c64 * ti - s64 * tr
    sums[...] = jnp.zeros_like(sums)

    def chunk(r, i, sr, si):
        ber = lead[0:SEG, :]
        bei = lead[SEG : 2 * SEG, :]
        ber = jnp.concatenate([ber, ber], axis=0)
        bei = jnp.concatenate([bei, bei], axis=0)
        qq = q[r, :]
        gr = g[r, 0:CH] + qq * ber
        gi = g[r, CH:] + qq * bei
        ct, st = turns(tab, i, 2)
        l = lam[r, :]
        keep_carry = wide(nf[r, :])
        adm = 1.0 - l
        xr = pre[r, 0:CH]
        xi = pre[r, CH:]
        zr = jax.nn.sigmoid(xr)
        zi = jax.nn.sigmoid(xi)
        ur = gr * ct - gi * st
        ui = gr * st + gi * ct
        dot_s = gr * sr + gi * si
        turn = gi * sr - gr * si
        back_lam = keep_carry * dot_s - (ur * (xr * zr) + ui * (xi * zi))
        bf = back_lam * l * adm
        bpf[r, :] = bf.astype(BF16)
        bpi[r, 0:CH] = (adm * ur * (zr * (1.0 + xr * (1.0 - zr)))).astype(BF16)
        bpi[r, CH:] = (adm * ui * (zi * (1.0 + xi * (1.0 - zi)))).astype(BF16)
        rot = l * keep_carry * turn
        sums[0:SEG, :] += bf[0:SEG, :] + bf[SEG : 2 * SEG, :]
        sums[SEG : 2 * SEG, :] += rot[0:SEG, :] + rot[SEG : 2 * SEG, :]

    chunk(
        pl.ds(0, 2 * SEG),
        0,
        jnp.concatenate([enter[0:SEG, :], t[0:SEG, 0:CH]], axis=0),
        jnp.concatenate([enter[SEG : 2 * SEG, :], t[0:SEG, CH:]], axis=0),
    )

    def step(r, i):
        before = pl.ds(pl.multiple_of(i * 16 - SEG, SEG), 16)
        chunk(r, i, t[before, 0:CH], t[before, CH:])

    loop(ROWS // 16, 16, step, 1)
    cp("out", bpi, bpi_h)
    cp("out", bpf, bpf_h)
    cp.wait("b")
    n = normed[...]
    put_grad(tn(bpi[:, 0:CH], n), 0, mine, other)
    put_grad(tn(bpi[:, CH:], n), 1, mine, other)
    put_grad(tn(bpf[...], n), 2, mine, other)
    cp("out", other, other_h)
    cp("out", mine, mine_h)
    total_b = jnp.sum(sums[0:SEG, :], axis=0, keepdims=True)
    total_r = jnp.sum(sums[SEG : 2 * SEG, :], axis=0, keepdims=True)
    sums[...] = jnp.zeros_like(sums)
    sums[0:1, :] = total_b
    sums[1:2, :] = total_r
    lead[0:SEG, :] = exact(sums[0:SEG, :], perm[...])
    cp("out", lead.at[pl.ds(0, SEG)], parts_h)
    cp.finish()


def k_input(me, x_h, keep_h, gain_h, bm_h, bpi_h, bpf_h, bpg_h, gpart_h, parts_h, *rest):
    pieces = rest[:8]
    grad_h, small_h = rest[8:10]
    w, x, keep, gain, bm, bpi, bpf, bpg, gpart, parts, bn, grad, gsum, small, sems = rest[10:]
    cp = Copies(sems)
    cp("a", bpi_h, bpi)
    fetch_mix(cp, "a", pieces, (0, 2), w, 0)
    cp("a", bpf_h, bpf)
    cp("a", bpg_h, bpg)
    fetch_mix(cp, "a", pieces, (2, 3), w, 2)
    cp("b", x_h, x)
    cp("b", keep_h, keep)
    cp("b", gain_h, gain)
    cp("b", bm_h, bm)
    cp("b", gpart_h, gpart)
    cp("b", parts_h, parts)
    cp.wait("a")
    bn[...] = (
        nn(bpi[...], w[0:2].reshape(2 * CH, D))
        + nn(bpf[...], w[2])
        + nn(bpg[...], w[3:5].reshape(2 * CH, D))
    )
    gsum[...] = jnp.zeros_like(gsum)
    cp.wait("b")

    def norm(r, i):
        v = x[r, :].astype(F32)
        b = bn[r, :]
        rs = lax.rsqrt(jnp.mean(v * v, axis=-1, keepdims=True) + EPS)
        kp = keep[r, :1]
        gsum[...] += jnp.sum(b * v * (rs * kp), axis=0, keepdims=True)
        u1 = b * gain[...] * kp
        m = jnp.mean(u1 * v, axis=-1, keepdims=True)
        grad[r, :] = (bm[r, :] + rs * u1 - v * (rs * rs * rs * m)).astype(BF16)

    loop(8, 64, norm)
    first = me[0] % 2 == 0
    small[...] = jnp.zeros_like(small)
    for i, part in enumerate((gsum, gpart)):
        own, rest_half = part[:, :H], part[:, H:]
        small[2 * i : 2 * i + 1, :] = jnp.where(first, own, rest_half)
        small[2 * i + 1 : 2 * i + 2, :] = jnp.where(first, rest_half, own)
    small[4:6, :] = parts[0:2, :]
    cp("out", small, small_h)
    cp("out", grad, grad_h)
    cp.finish()


ANY = pl.BlockSpec(memory_space=pl.ANY)
SM = pl.BlockSpec(memory_space=pltpu.SMEM)


def call(kernel, args, outs, scratch, copies, scalar=True, vmem=48, us=5):
    specs = [ANY] * len(args)
    if scalar:
        specs[0] = SM
    return pl.pallas_call(
        kernel,
        in_specs=specs,
        out_specs=[ANY] * len(outs),
        out_shape=[jax.ShapeDtypeStruct(s, t) for s, t in outs],
        scratch_shapes=[pltpu.VMEM(s, t) for s, t in scratch] + [pltpu.SemaphoreType.DMA((copies,))],
        compiler_params=pltpu.CompilerParams(vmem_limit_bytes=vmem * 1024 * 1024),
        name=kernel.__name__,
        cost_estimate=pl.CostEstimate(flops=us, bytes_accessed=us, transcendentals=0),
    )(*args)


def device(z, y, c):
    return ((z % NZ) * NY + (y % NY)) * 2 + c


EVERY = [(z, y, c) for z in range(NZ) for y in range(NY) for c in range(2)]


def swap_core(v):
    return lax.ppermute(v, "ch", [(device(z, y, c), device(z, y, 1 - c)) for z, y, c in EVERY])


def move_z(v, k):
    return lax.ppermute(v, "ch", [(device(z, y, c), device(z + k, y, c)) for z, y, c in EVERY])


def move_y(v, k):
    return lax.ppermute(v, "ch", [(device(z, y, c), device(z, y + k, c)) for z, y, c in EVERY])


def move_x(v, k):
    return lax.ppermute(v, "dp", [(i, (i + k) % NX) for i in range(NX)])


def partner(i, c, k):
    return (i, i ^ 1, 3 - i, i ^ 2)[SWAP[k] if c else k]


def exchange_z(v, k):
    return lax.ppermute(v, "ch", [(device(z, y, c), device(partner(z, c, k), y, c)) for z, y, c in EVERY])


def exchange_y(v, k):
    return lax.ppermute(v, "ch", [(device(z, y, c), device(z, partner(y, c, k), c)) for z, y, c in EVERY])


def exchange_x(v, k):
    return lax.ppermute(
        v,
        ("dp", "ch"),
        [(x * 32 + device(z, y, c), partner(x, c, k) * 32 + device(z, y, c)) for x in range(NX) for z, y, c in EVERY],
    )


def after(value, *others):
    return lax.optimization_barrier((value,) + others)[0]


def gather_chip(pack, core):
    got = swap_core(pack[:, :, H:])
    mine = pack[:, :, :H]
    return jnp.where(
        core == 0, jnp.concatenate([mine, got], axis=1), jnp.concatenate([got, mine], axis=1)
    )


def gather_line(v, move):
    return [v] + [move(v, -k) for k in (1, 2, 3)]


def gather_ring(v, exchange):
    one = exchange(v, 1)
    return [v, one, exchange(v, 2), exchange(one, 2)]


def gather_summary(summary, beside):
    pair = jnp.concatenate([summary, swap_core(summary)], axis=0)
    line = after(jnp.concatenate(gather_line(pair, move_z), axis=0), beside)
    return gather_line(line, move_y), line


def add4(own, near, far, near_too):
    a, b, c, d = [v.astype(F32) for v in (own, near, far, near_too)]
    return (a + c) + (b + d)


def reduce_core(mine, other):
    return (mine.astype(F32) + swap_core(other).astype(F32)).astype(BF16)


def reduce_pieces(pieces, move):
    return add4(pieces[0], *[move(pieces[k], k) for k in (1, 2, 3)])


def reduce_outer(pieces, exchange):
    return add4(pieces[0], *[exchange(pieces[k], k) for k in (1, 3, 2)])


def reduce_half(slots, exchange):
    return (slots[:2].astype(F32) + exchange(slots[2:], 1).astype(F32)).astype(BF16)


def reduce_last(two, exchange):
    return two[0].astype(F32) + exchange(two[1], 2).astype(F32)


def finish(keep, send, core):
    got = swap_core(send)
    return jnp.where(
        core == 0, jnp.concatenate([keep, got], axis=-1), jnp.concatenate([got, keep], axis=-1)
    )


def finish_units(own, core):
    keep = jnp.where(core == 0, own[:, :12], own[:, 12:])
    send = jnp.where(core == 0, own[:, 12:], own[:, :12])
    return finish(keep, send, core)


def finish_mlp(chip, core, xi):
    groups = jnp.stack(gather_line(chip, move_x))
    groups = jnp.concatenate([groups, groups[:3]], axis=0)
    groups = lax.dynamic_slice_in_dim(groups, (NX - xi) % NX, NX, axis=0)
    kinds = groups.reshape(3, 2, 48, H)
    keep = jnp.where(core == 0, kinds[:, 0], kinds[:, 1])
    send = jnp.where(core == 0, kinds[:, 1], kinds[:, 0])
    return finish(keep, send, core).astype(F32)


def halves(rows):
    hi = lax.reduce_precision(rows, 8, 7)
    return jnp.concatenate([hi, lax.reduce_precision(rows - hi, 8, 7)], axis=0).astype(BF16)


def end_phase(pieces, small, move, reduce):
    units, rows = pieces[0].shape[0], pieces[0].shape[0] * pieces[0].shape[1]
    tail = halves(small)
    total = reduce([jnp.concatenate([p.reshape(rows, H), tail], axis=0) for p in pieces], move)
    return total[:rows].astype(BF16).reshape(units, -1, H), total[rows : rows + 8] + total[rows + 8 :]


def to_steps(v):
    return v.reshape(SEG, STEPS, *v.shape[1:]).swapaxes(0, 1).reshape(v.shape)


def from_steps(v):
    return v.reshape(STEPS, SEG, *v.shape[1:]).swapaxes(0, 1).reshape(v.shape)


def shards(
    block_input, gain_mix, w_input, w_forget, w_outgate, bias_forget, rotation, w_out,
    gain_mlp, w_gate, w_up, w_down, seq_lengths, pad_mask, cotangent,
):
    place = lax.axis_index("ch").astype(jnp.int32)
    xi = lax.axis_index("dp").astype(jnp.int32)
    core = place % 2
    y = (place // 2) % NY
    z = place // (2 * NY)

    def own_first(v):
        return jnp.where(core == 0, v, jnp.concatenate([v[..., H:], v[..., :H]], axis=-1))

    def parts(w):
        return w.T.reshape(12, 2, D).swapaxes(0, 1)

    vec = jnp.concatenate([bias_forget, rotation])
    hi = lax.reduce_precision(vec, 8, 7)
    mid = lax.reduce_precision(vec - hi, 8, 7)
    extra = jnp.concatenate([hi, mid, vec - hi - mid]).astype(BF16)
    mix_pack = own_first(
        jnp.concatenate(
            [
                parts(w_input),
                w_forget.T[None],
                parts(w_outgate),
                w_out.reshape(12, 2, D).swapaxes(0, 1),
            ],
            axis=0,
        )
    )
    mlp_pack = own_first(jnp.stack([w_gate.T, w_up.T, w_down]))
    rows = MIX_U * UNIT
    mix_chip = gather_chip(mix_pack, core).reshape(rows, H)
    mix_chip = jnp.concatenate([mix_chip, jnp.pad(extra[None], ((0, 7), (0, H - 72)))], axis=0)
    mlp_chip = gather_chip(mlp_pack, core)
    mix_line = gather_line(mix_chip, move_y)
    mlp_line = gather_line(mlp_chip, move_z)
    mix_line, mlp_line, block_input, cotangent, seq_lengths, pad_mask = lax.optimization_barrier(
        (mix_line, mlp_line, block_input, cotangent, seq_lengths, pad_mask)
    )
    mix_line = jnp.concatenate(
        [jnp.concatenate([f[:rows].reshape(MIX_U, UNIT, H) for f in mix_line], axis=1).reshape(VEC, H)]
        + [f[rows:] for f in mix_line],
        axis=0,
    )
    mix_own = gather_ring(mix_line, exchange_z)
    mlp_own = gather_ring(jnp.concatenate(mlp_line, axis=1), exchange_y)

    j = jnp.arange(CH, dtype=jnp.int32)
    rest = j % 96
    ky, tail = rest // UNIT, rest % UNIT
    flip = jnp.where(core == 0, jnp.array([0, 1, 3, 2]), jnp.array([0, 3, 1, 2])).astype(jnp.int32)
    where_to = jnp.bitwise_xor(jnp.repeat(flip, 96), z) * 96 + ((ky + y) % NY) * UNIT + tail
    perm = (where_to[:, None] == j[None, :]).astype(F32)

    lengths = seq_lengths[0]
    ends = jnp.sum(jnp.where(jnp.arange(8)[:, None] >= jnp.arange(8)[None, :], lengths[None, :], 0), axis=1)
    starts = ends - lengths
    r = jnp.arange(ROWS, dtype=jnp.int32)
    position = place * ROWS + (r % SEG) * STEPS + r // SEG
    first = jnp.any(position[:, None] == starts[None, :], axis=1)
    nf = jnp.broadcast_to(1.0 - first.astype(F32)[:, None], (ROWS, 128))
    keep = jnp.broadcast_to(to_steps(pad_mask.astype(F32))[:, None], (ROWS, 128))

    x = own_first(to_steps(block_input))
    ups = own_first(to_steps(cotangent)) * keep[:, :1].astype(BF16)
    gain1 = own_first(gain_mix)[None]
    gain2 = own_first(gain_mlp)[None]
    number = jnp.where(core == 0, jnp.array([0, 1, 3, 2]), jnp.array([0, 2, 3, 1])).astype(jnp.int32)
    number = [jnp.take(number, jnp.bitwise_xor(xi, g)) for g in range(NX)]
    slot = [jnp.where((k == 1) | (k == 2), 3 - k, k) for k in number]
    me = jnp.stack([place, xi] + slot + number)

    wide_f = ((ROWS, D), F32)
    wide_b = ((ROWS, D), BF16)
    half_f = ((ROWS, CH), F32)
    half_b = ((ROWS, CH), BF16)
    lanes = ((ROWS, 128), F32)
    tab_s = ((TAB, CH), F32)
    perm_s = ((CH, CH), F32)
    few = ((SEG, CH), F32)
    pair = ((2 * SEG, CH), F32)
    gain_s = ((1, D), F32)
    order_s = ((32 * SEG, CH), F32)

    (normed,) = call(
        k_norm, [x, keep, gain1], [wide_b], [wide_b, lanes, gain_s, wide_b], 4, scalar=False, us=3
    )
    mix_own[3] = after(mix_own[3], normed, ups, nf, perm)
    mix_w = mix_own + [swap_core(p) for p in mix_own]
    pre, s, lam, cum, tab, summary = call(
        k_project,
        [me, normed, nf, perm] + mix_w,
        [wide_f, wide_f, half_f, half_f, tab_s, few],
        [((3, CH, D), BF16), wide_b, lanes, perm_s, ((256, H), BF16), wide_f, half_f, wide_f, half_f, half_f, tab_s,
         few],
        44,
        us=6,
    )
    mlp_own, _ = lax.optimization_barrier((mlp_own, summary))
    mlp_w = mlp_own + [swap_core(p) for p in mlp_own]
    (pg,) = call(k_gate, [normed] + mix_w, [wide_f], [((2, CH, D), BF16), wide_b, wide_f], 20, scalar=False, us=3)
    before, _ = gather_summary(summary, pg)
    hidden = ((ROWS, FF), BF16)
    mlp_g = ((4, 3, 4 * 96, H), BF16)
    mlp_s = ((12, 4 * 96, H), BF16)
    t, sg, gated, mixed, enter, out, bmlp, mlp_mine, mlp_other = call(
        k_ffn,
        [me] + before + [tab, perm, s, cum, pg, x, gain2, ups] + mix_w + mlp_w,
        [wide_f, wide_f, wide_b, wide_f, pair, wide_b, wide_f, mlp_g, mlp_g],
        [((2, CH, D), BF16), ((3, FF, D), BF16), order_s, tab_s, perm_s, wide_f, half_f, wide_f, wide_b, gain_s,
         wide_b, few, pair, wide_b, wide_f, wide_b, hidden, hidden, hidden, wide_b, wide_f, mlp_s, mlp_s],
        112,
        vmem=44,
        us=20,
    )
    bm, gpart, bgt, g, q, summary_back, bml = call(
        k_back,
        [me, bmlp, mixed, ups, gain2, sg, lam, nf, tab, perm] + mix_w,
        [wide_f, gain_s, wide_f, wide_f, half_f, few, wide_b],
        [((2, CH, D), BF16), wide_f, wide_f, wide_b, gain_s, wide_f, half_f, lanes, tab_s, perm_s, wide_f, wide_f,
         wide_f, half_f, wide_b, few, gain_s],
        38,
        us=6,
    )
    mid_g = ((4, 4, 96, H), BF16)
    bpg, mid_mine, mid_other = call(
        k_mid,
        [bgt, t, sg, tab, normed, gated, bml],
        [wide_b, mid_g, mid_g],
        [wide_f, wide_f, wide_f, tab_s, wide_b, wide_b, wide_b, wide_b, mid_g, mid_g],
        12,
        scalar=False,
        us=5,
    )
    behind, line = gather_summary(summary_back, bpg)
    mlp_mine = after(mlp_mine, line)
    mlp_both = reduce_core(mlp_mine, mlp_other)
    behind[0] = after(behind[0], mlp_both)
    end_g = ((4, 3, 96, H), BF16)
    bpi, bpf, vec_parts, end_mine, end_other = call(
        k_last,
        [me] + behind + [tab, perm, g, q, lam, nf, t, enter, pre, normed],
        [wide_b, half_b, few, end_g, end_g],
        [order_s, tab_s, perm_s, wide_f, half_f, half_f, lanes, wide_f, pair, wide_f, wide_b, wide_b, half_b, end_g,
         end_g, pair, pair],
        50,
        us=6,
    )
    end_both = reduce_core(end_mine, end_other)
    grad_input, small = call(
        k_input,
        [me, x, keep, gain1, bm, bpi, bpf, bpg, gpart, vec_parts] + mix_w,
        [wide_b, few],
        [((5, CH, D), BF16), wide_b, lanes, gain_s, wide_f, wide_b, half_b, wide_b, gain_s, few, wide_f, wide_b, gain_s,
         few],
        54,
        us=5,
    )
    mid_both = after(reduce_core(mid_mine, mid_other), *behind)
    mlp_two = reduce_half(mlp_both, exchange_x)
    small = after(small, end_both)
    mid_line = reduce_outer([mid_both[k] for k in range(4)], exchange_z).astype(BF16).reshape(4, 4, UNIT, H)
    end_both = after(end_both, mid_line)
    end_line, small = end_phase([end_both[k] for k in range(4)], small + swap_core(small), exchange_z, reduce_outer)
    mid_line, mlp_two = lax.optimization_barrier((mid_line, mlp_two))
    mlp_own = reduce_last(mlp_two, exchange_x).astype(BF16).reshape(3, 4, 96, H)
    end_line, mlp_own = lax.optimization_barrier((end_line, mlp_own))
    end_line = end_line.reshape(3, 4, UNIT, H)
    mid_own = reduce_pieces([mid_line[:, k] for k in range(4)], move_y).astype(BF16)
    end_own, small = end_phase([end_line[:, k] for k in range(4)], small, move_y, reduce_pieces)
    mlp_line = reduce_outer([mlp_own[:, k] for k in range(4)], exchange_y).astype(BF16).reshape(3, 4, UNIT, H)
    mid_own = reduce_pieces([mid_own] * 4, move_x)
    grads_mid = finish_units(mid_own, core)
    end_own = jnp.concatenate([end_own.reshape(3 * UNIT, H), halves(small)], axis=0)
    total = reduce_pieces([end_own] * 4, move_x)
    grads_end = finish_units(total[: 3 * UNIT].reshape(3, UNIT, H), core)
    small = total[3 * UNIT : 3 * UNIT + 8] + total[3 * UNIT + 8 :]
    mlp_chip = reduce_pieces([mlp_line[:, k] for k in range(4)], move_z).astype(BF16)
    grads_mlp = finish_mlp(mlp_chip, core, xi)
    bias_grad = lax.dynamic_slice(small[4], (place * 12,), (12,))
    rot_grad = lax.dynamic_slice(small[5], (place * 12,), (12,))

    def together(re_im):
        return re_im.swapaxes(0, 1).reshape(UNIT, D)

    return (
        from_steps(own_first(out)),
        from_steps(own_first(grad_input)),
        small[0:2].reshape(D),
        together(grads_end[0:2]).T,
        grads_end[2].T,
        together(grads_mid[0:2]).T,
        bias_grad,
        rot_grad,
        together(grads_mid[2:4]),
        small[2:4].reshape(D),
        grads_mlp[0].T,
        grads_mlp[1].T,
        grads_mlp[2],
    )


def solution(mesh):
    rows = P(("dp", "ch"), None)
    cols = P(None, "ch")
    return jax.shard_map(
        shards,
        mesh=mesh,
        in_specs=(
            rows, P(), cols, cols, cols, P("ch"), P("ch"), P("ch", None), P(), cols, cols,
            P("ch", None), P("dp", None), P(("dp", "ch")), rows,
        ),
        out_specs=(
            rows, rows, P(), cols, cols, cols, P("ch"), P("ch"), P("ch", None), P(), cols, cols,
            P("ch", None),
        ),
        check_vma=False,
    )
```

```python
import jax
import jax.numpy as jnp
from jax import lax
from jax.experimental import pallas as pl
from jax.experimental.pallas import tpu as pltpu
from jax.sharding import PartitionSpec as P

EPS = 1e-06
F32 = jnp.float32
BF16 = jnp.bfloat16

ROWS = 512
D = 768
H = 384
CH = 384
FF = 1536
SEG = 8
STEPS = ROWS // SEG
NZ, NY, NX = 4, 4, 4
UNIT = 24
MIX_U = 7
VEC = 96 * MIX_U
COS, SIN, C64, S64, C512, S512, BIAS = 0, 64, 128, 129, 130, 131, 132
TAB = 136
SWAP = (0, 2, 1, 3)


def nt(a, b):
    return lax.dot_general(a, b, (((1,), (1,)), ((), ())), preferred_element_type=F32)


def nn(a, b):
    return lax.dot_general(a, b, (((1,), (0,)), ((), ())), preferred_element_type=F32)


def tn(a, b):
    return lax.dot_general(a, b, (((0,), (0,)), ((), ())), preferred_element_type=F32)


def exact(a, b):
    return lax.dot_general(
        a, b, (((1,), (0,)), ((), ())), precision=lax.Precision.HIGHEST, preferred_element_type=F32
    )


def exact_t(a, b):
    return lax.dot_general(
        a, b, (((1,), (1,)), ((), ())), precision=lax.Precision.HIGHEST, preferred_element_type=F32
    )


def wide(col):
    return jnp.concatenate([col, col, col], axis=1)


def loop(count, size, body, start=0):
    def step(i, _):
        body(pl.ds(pl.multiple_of(i * size, size), size), i)
        return 0

    lax.fori_loop(start, count, step, 0)


class Copies:
    def __init__(self, sems):
        self.sems = sems
        self.used = 0
        self.open = {}

    def __call__(self, name, src, dst):
        copy = pltpu.make_async_copy(src, dst, self.sems.at[self.used])
        self.used += 1
        copy.start()
        self.open.setdefault(name, []).append(copy)

    def wait(self, *names):
        for name in names:
            for copy in self.open.pop(name):
                copy.wait()

    def finish(self):
        self.wait(*list(self.open))


def fetch_mix(cp, name, pieces, units, scratch, at):
    for u in range(units[0], units[0] + units[1]):
        for half in range(2):
            for k in range(4):
                cp(
                    name,
                    pieces[half * 4 + (SWAP[k] if half else k)].at[pl.ds(96 * u, 96)],
                    scratch.at[at + u - units[0], pl.ds(96 * k, 96), pl.ds(H * half, H)],
                )


def fetch_mlp(cp, name, pieces, kind, scratch, at=None):
    for half in range(2):
        for k in range(4):
            cp(
                name,
                pieces[half * 4 + (SWAP[k] if half else k)].at[kind],
                scratch.at[kind if at is None else at, pl.ds(CH * k, CH), pl.ds(H * half, H)],
            )


def put_grad(grad, unit, mine, other):
    low = grad.astype(BF16)
    for k in range(4):
        mine[k, unit] = low[96 * k : 96 * k + 96, :H]
        other[SWAP[k], unit] = low[96 * k : 96 * k + 96, H:]


def turns(tab, i, steps):
    rows = []
    for base in (COS, SIN):
        parts = [
            jnp.broadcast_to(tab[pl.ds(base + i * steps + s, 1), :], (SEG, CH)) for s in range(steps)
        ]
        rows.append(parts[0] if steps == 1 else jnp.concatenate(parts, axis=0))
    return rows


def row(ref, i):
    return ref[i : i + 1, :]


def summaries(cp, me, pieces, order):
    core = me[0] % 2
    y = (me[0] // 2) % NY
    z = me[0] // (2 * NY)
    for kz in range(NZ):
        for ky in range(NY):
            for kc in range(2):
                place = (((z + kz) % NZ) * NY + (y + ky) % NY) * 2 + (core + kc) % 2
                cp(
                    "order",
                    pieces[ky].at[pl.ds((kz * 2 + kc) * SEG, SEG)],
                    order.at[pl.ds(pl.multiple_of(place * SEG, SEG), SEG)],
                )


def k_pack(me, in_h, forget_h, gate_h, out_h, ffn_gate_h, ffn_up_h, ffn_down_h, mix_mine_h, mix_other_h, mlp_mine_h, mlp_other_h, *rest):
    w_in, w_forget, w_gate, w_out, w, mix_mine, mix_other, mlp_mine, mlp_other, sems = rest
    cp = Copies(sems)
    cp("mix", in_h, w_in)
    cp("mix", forget_h, w_forget)
    cp("mix", gate_h, w_gate)
    cp("mix", out_h, w_out)
    for i, ref in enumerate((ffn_gate_h, ffn_up_h, ffn_down_h)):
        cp("mlp", ref, w.at[i])
    first = me[0] % 2 == 0

    def put(value, mine, other):
        left, right = value[:, :H], value[:, H:]
        mine[...] = jnp.where(first, left, right).astype(BF16)
        other[...] = jnp.where(first, right, left).astype(BF16)

    def pick(columns, factor, offset):
        at = lax.broadcasted_iota(jnp.int32, (16, columns), 0) * factor + offset
        return jnp.where(at == lax.broadcasted_iota(jnp.int32, (16, columns), 1), 1.0, 0.0).astype(BF16)

    every_other = (pick(24, 2, 0), pick(24, 2, 1))
    each = pick(12, 1, 0)
    cp.wait("mix")
    for unit, ref in ((0, w_in), (3, w_gate), (5, w_out)):
        for part in range(2):
            put(nn(every_other[part], ref[...]), mix_mine.at[unit + part], mix_other.at[unit + part])
    put(nn(each, w_forget[...]), mix_mine.at[2], mix_other.at[2])
    cp("out", mix_other, mix_other_h)
    cp("out", mix_mine, mix_mine_h)
    cp.wait("mlp")
    for i in range(3):
        put(w[i].astype(F32), mlp_mine.at[i], mlp_other.at[i])
    cp("out", mlp_other, mlp_other_h)
    cp("out", mlp_mine, mlp_mine_h)
    cp.finish()


def k_norm(x_h, keep_h, gain_h, normed_h, x, keep, gain, normed, sems):
    cp = Copies(sems)
    cp("x", x_h, x)
    cp("x", keep_h, keep)
    cp("x", gain_h, gain)
    cp.wait("x")

    def norm(r, i):
        v = x[r, :].astype(F32)
        rs = lax.rsqrt(jnp.mean(v * v, axis=-1, keepdims=True) + EPS) * keep[r, :1]
        normed[r, :] = (v * rs * gain[...]).astype(BF16)

    loop(8, 64, norm)
    cp("out", normed, normed_h)
    cp.finish()


def k_project(me, normed_h, nf_h, perm_h, *rest):
    pieces = rest[:8]
    pre_h, s_h, lam_h, cum_h, tab_h, summary_h = rest[8:14]
    w, normed, nf, perm, vecs, pre, pf, s, lam, cum, tab, sums, sems = rest[14:]
    cp = Copies(sems)
    for i in range(8):
        cp("vecs", pieces[i].at[pl.ds(VEC, 32)], vecs.at[pl.ds(32 * i, 32)])
    cp("w", normed_h, normed)
    fetch_mix(cp, "w", pieces, (0, 3), w, 0)
    cp("nf", perm_h, perm)
    cp("nf", nf_h, nf)

    cp.wait("vecs")
    group = lax.broadcasted_iota(jnp.int32, (32, 256), 0)
    half = (group + me[0]) % 2
    kz = group // 8
    kz = jnp.where((half == 1) & (kz > 0) & (kz < 3), 3 - kz, kz)
    source = 32 * (half * 4 + kz) + 8 * ((group // 2) % 4)
    choose = jnp.where(source == lax.broadcasted_iota(jnp.int32, (32, 256), 1), 1.0, 0.0).astype(BF16)
    values = nn(choose, vecs[...])[:, :128].astype(BF16)
    sub = lax.broadcasted_iota(jnp.int32, (128, CH), 0)
    same = (sub % 12 == lax.broadcasted_iota(jnp.int32, (128, CH), 1) % 12) & (sub < 72)
    hit = lax.broadcasted_iota(jnp.int32, (32, CH), 0) == lax.broadcasted_iota(jnp.int32, (32, CH), 1) // 12
    found = []
    for v in range(2):
        pick = jnp.where(same & ((sub % 24) // 12 == v), 1.0, 0.0).astype(BF16)
        found.append(jnp.sum(jnp.where(hit, nn(values, pick), 0.0), axis=0, keepdims=True))
    bias, rot = found
    few = lax.broadcasted_iota(jnp.int32, (SEG, CH), 0)
    one = few.astype(F32) * rot
    eight = one * 8.0
    far = jnp.where(few < 2, float(STEPS), float(ROWS)) * rot
    c_one, s_one, c_eight, s_eight = jnp.cos(one), jnp.sin(one), jnp.cos(eight), jnp.sin(eight)
    for i in range(SEG):
        ca, sa = c_eight[i : i + 1], s_eight[i : i + 1]
        tab[COS + SEG * i : COS + SEG * i + SEG, :] = ca * c_one - sa * s_one
        tab[SIN + SEG * i : SIN + SEG * i + SEG, :] = sa * c_one + ca * s_one
    cos, sin = jnp.cos(far), jnp.sin(far)
    c64, s64 = cos[0:1], sin[0:1]
    cp.wait("nf")
    far = exact(jnp.where(few % 2 == 0, cos, sin), perm[...])
    tab[C64:TAB, :] = jnp.zeros((SEG, CH), F32)
    tab[C64 : C64 + 1, :] = c64
    tab[S64 : S64 + 1, :] = s64
    tab[C512 : C512 + 1, :] = far[2:3]
    tab[S512 : S512 + 1, :] = far[3:4]
    cp("out", tab, tab_h)

    cp.wait("w")
    n = normed[...]
    pre[:, 0:CH] = nt(n, w[0])
    pre[:, CH:] = nt(n, w[1])
    pf[...] = nt(n, w[2])
    cp("out", pre, pre_h)

    def step(t, carry):
        sr, si, p = carry
        r = pl.ds(pl.multiple_of(t * SEG, SEG), SEG)
        l = jax.nn.sigmoid(pf[r, :] + bias)
        a = l * wide(nf[r, :])
        adm = 1.0 - l
        vr = pre[r, 0:CH]
        vi = pre[r, CH:]
        vr = adm * vr * jax.nn.sigmoid(vr)
        vi = adm * vi * jax.nn.sigmoid(vi)
        ct, st = turns(tab, t, 1)
        sr = a * sr + (vr * ct + vi * st)
        si = a * si + (vi * ct - vr * st)
        p = a * p
        lam[r, :] = l
        s[r, 0:CH] = sr
        s[r, CH:] = si
        cum[r, :] = p
        return sr, si, p

    zero = jnp.zeros((SEG, CH), F32)
    sr, si, p = lax.fori_loop(0, STEPS, step, (zero, zero, zero + 1.0), unroll=4)
    cp("out", s, s_h)
    cp("out", lam, lam_h)
    cp("out", cum, cum_h)
    er = jnp.zeros((1, CH), F32)
    ei = jnp.zeros((1, CH), F32)
    pt = jnp.ones((1, CH), F32)
    for b in range(SEG):
        pb = p[b : b + 1]
        tr = sr[b : b + 1] + pb * er
        ti = si[b : b + 1] + pb * ei
        er = c64 * tr - s64 * ti
        ei = c64 * ti + s64 * tr
        pt = pt * pb
    sums[...] = jnp.zeros_like(sums)
    sums[0:1, :] = pt
    sums[1:2, :] = er
    sums[2:3, :] = ei
    sums[...] = exact(sums[...], perm[...])
    cp("out", sums, summary_h)
    cp.finish()


def k_middle(
    me, gat0, gat1, gat2, gat3, tab_h, perm_h, s_h, cum_h, normed_h, x_h, gain_h, ups_h, lam_h, nf_h, *rest
):
    mix_p, mlp_p = rest[:8], rest[8:16]
    (t_h, enter_h, act_h, mixed_h, bm_h, g_h, q_h, bpg_h, gpart_h, gdot_h, summary_h, mine_h, other_h, mid_mine_h,
     mid_other_h) = rest[16:31]
    (wg, wo, w, order, tab, perm, s, cum, normed, x, gain, ups, lam, nf, sums, enter, pg, gated, mixed, nm, act, bg, bu,
     mine, other, bm, bml, g, q, bpg, gsum, gdot, mid_mine, mid_other, sems) = rest[31:]
    cp = Copies(sems)
    cp("gate", normed_h, normed)
    fetch_mix(cp, "gate", mix_p, (3, 2), wg, 0)
    summaries(cp, me, (gat0, gat1, gat2, gat3), order)
    cp("order", tab_h, tab)
    cp("order", perm_h, perm)
    cp("s", s_h, s)
    cp("s", cum_h, cum)
    fetch_mix(cp, "wo", mix_p, (5, 2), wo, 0)
    cp("x", x_h, x)
    cp("x", gain_h, gain)
    fetch_mlp(cp, "w_gate", mlp_p, 0, w)
    fetch_mlp(cp, "w_up", mlp_p, 1, w)
    cp("ups", ups_h, ups)
    fetch_mlp(cp, "w_down", mlp_p, 2, w)
    cp("lam", lam_h, lam)
    cp("lam", nf_h, nf)

    cp.wait("order", "gate")
    pg[...] = nt(normed[...], wg[...].reshape(2 * CH, D))
    c512, s512 = row(tab, C512), row(tab, S512)
    c64, s64 = row(tab, C64), row(tab, S64)
    er = jnp.zeros((1, CH), F32)
    ei = jnp.zeros((1, CH), F32)
    for d in range(31):
        pd = row(order, 8 * d)
        nr = row(order, 8 * d + 1) + pd * (c512 * er - s512 * ei)
        ni = row(order, 8 * d + 2) + pd * (c512 * ei + s512 * er)
        er = jnp.where(d < me[0], nr, er)
        ei = jnp.where(d < me[0], ni, ei)
    sums[...] = jnp.zeros_like(sums)
    sums[0:1, :] = er
    sums[1:2, :] = ei
    back = exact_t(sums[...], perm[...])
    er = back[0:1, :]
    ei = back[1:2, :]
    cp.wait("s")
    last = ROWS - SEG
    for b in range(SEG):
        enter[b : b + 1, :] = er
        enter[SEG + b : SEG + b + 1, :] = ei
        pb = row(cum, last + b)
        tr = s[last + b : last + b + 1, 0:CH] + pb * er
        ti = s[last + b : last + b + 1, CH:] + pb * ei
        er = c64 * tr - s64 * ti
        ei = c64 * ti + s64 * tr
    cp("out", enter, enter_h)

    def fix(r, i):
        ber = enter[0:SEG, :]
        bei = enter[SEG : 2 * SEG, :]
        ber = jnp.concatenate([ber, ber], axis=0)
        bei = jnp.concatenate([bei, bei], axis=0)
        p = cum[r, :]
        sr = s[r, 0:CH] + p * ber
        si = s[r, CH:] + p * bei
        s[r, 0:CH] = sr
        s[r, CH:] = si
        ct, st = turns(tab, i, 2)
        gr = jax.nn.sigmoid(pg[r, 0:CH])
        gi = jax.nn.sigmoid(pg[r, CH:])
        pg[r, 0:CH] = gr
        pg[r, CH:] = gi
        gated[r, 0:CH] = ((sr * ct - si * st) * gr).astype(BF16)
        gated[r, CH:] = ((sr * st + si * ct) * gi).astype(BF16)

    loop(32, 16, fix)
    cp("out", s, t_h)
    cp.wait("wo")
    mixed[...] = nn(gated[...], wo[...].reshape(2 * CH, D))
    cp.wait("x")

    def norm(r, i):
        v = mixed[r, :] + x[r, :].astype(F32)
        mixed[r, :] = v
        rs = lax.rsqrt(jnp.mean(v * v, axis=-1, keepdims=True) + EPS)
        nm[r, :] = (v * rs * gain[...]).astype(BF16)

    loop(8, 64, norm)
    cp("out", mixed, mixed_h)
    n = nm[...]
    cp.wait("w_gate", "w_up", "ups", "w_down")
    up_low = ups[...]
    for k in range(4):
        cols = slice(CH * k, CH * k + CH)
        gp = nt(n, w[0, cols, :])
        up = nt(n, w[1, cols, :])
        ba = nt(up_low, w[2, cols, :])
        sg = jax.nn.sigmoid(gp)
        ga = gp * sg
        act[:, cols] = (ga * up).astype(BF16)
        bg[:, cols] = (ba * up * sg * (1.0 + gp * (1.0 - sg))).astype(BF16)
        bu[:, cols] = (ba * ga).astype(BF16)
    cp("out", act, act_h)
    for kind, (left, right) in enumerate(((bg, n), (bu, n), (act, up_low))):
        for k in range(4):
            grad = tn(left[:, CH * k : CH * k + CH], right)
            for j in range(4):
                part = jnp.concatenate(
                    [grad[96 * i + UNIT * j : 96 * i + UNIT * j + UNIT] for i in range(4)], axis=0
                ).astype(BF16)
                mine[kind * 4 + j, 96 * k : 96 * k + 96, :] = part[:, :H]
                other[kind * 4 + j, 96 * SWAP[k] : 96 * SWAP[k] + 96, :] = part[:, H:]
        for j in range(4):
            unit = kind * 4 + j
            cp("out", other.at[unit], other_h.at[me[6 + unit // 3], unit % 3])
            cp("out", mine.at[unit], mine_h.at[me[2 + unit // 3], unit % 3])
    bm[...] = nn(bg[...], w[0]) + nn(bu[...], w[1])
    gsum[...] = jnp.zeros_like(gsum)

    def norm_back(r, i):
        v = mixed[r, :]
        b = bm[r, :]
        rs = lax.rsqrt(jnp.mean(v * v, axis=-1, keepdims=True) + EPS)
        gsum[...] += jnp.sum(b * v * rs, axis=0, keepdims=True)
        u2 = b * gain[...]
        m = jnp.mean(u2 * v, axis=-1, keepdims=True)
        o = ups[r, :].astype(F32) + rs * u2 - v * (rs * rs * rs * m)
        bm[r, :] = o
        bml[r, :] = o.astype(BF16)

    loop(8, 64, norm_back)
    cp("out", bm, bm_h)
    cp("out", gsum, gpart_h)
    b = bml[...]
    g[...] = nt(b, wo[...].reshape(2 * CH, D))

    def gate(r, i):
        sr = s[r, 0:CH]
        si = s[r, CH:]
        ct, st = turns(tab, i, 2)
        gr = pg[r, 0:CH]
        gi = pg[r, CH:]
        br = g[r, 0:CH] * gr
        bi = g[r, CH:] * gi
        bpg[r, 0:CH] = (br * (sr * ct - si * st) * (1.0 - gr)).astype(BF16)
        bpg[r, CH:] = (bi * (sr * st + si * ct) * (1.0 - gi)).astype(BF16)
        g[r, 0:CH] = br * ct + bi * st
        g[r, CH:] = bi * ct - br * st

    loop(32, 16, gate)
    cp("out", bpg, bpg_h)
    cp.wait("lam")

    def step(i, carry):
        cr, ci, p = carry
        r = pl.ds(pl.multiple_of((STEPS - 1 - i) * SEG, SEG), SEG)
        a = lam[r, :] * wide(nf[r, :])
        gr = g[r, 0:CH] + cr
        gi = g[r, CH:] + ci
        g[r, 0:CH] = gr
        g[r, CH:] = gi
        q[r, :] = p
        return a * gr, a * gi, a * p

    zero = jnp.zeros((SEG, CH), F32)
    cr, ci, p = lax.fori_loop(0, STEPS, step, (zero, zero, zero + 1.0), unroll=4)
    cp("out", g, g_h)
    cp("out", q, q_h)
    er = jnp.zeros((1, CH), F32)
    ei = jnp.zeros((1, CH), F32)
    pt = jnp.ones((1, CH), F32)
    for i in range(SEG - 1, -1, -1):
        pb = p[i : i + 1, :]
        tr = cr[i : i + 1, :] + pb * er
        ti = ci[i : i + 1, :] + pb * ei
        er = c64 * tr + s64 * ti
        ei = c64 * ti - s64 * tr
        pt = pt * pb
    sums[...] = jnp.zeros_like(sums)
    sums[0:1, :] = pt
    sums[1:2, :] = er
    sums[2:3, :] = ei
    sums[...] = exact(sums[...], perm[...])
    cp("out", sums, summary_h)

    b = bml[...]
    put_grad(tn(gated[:, 0:CH], b), 2, mid_mine, mid_other)
    put_grad(tn(gated[:, CH:], b), 3, mid_mine, mid_other)
    n = normed[...]
    dots = []
    for i in range(2):
        grad = tn(bpg[:, CH * i : CH * i + CH], n)
        put_grad(grad, i, mid_mine, mid_other)
        dots.append(jnp.sum(grad * wg[i].astype(F32), axis=0, keepdims=True))
    gdot[...] = dots[0] + dots[1]
    cp("out", mid_other, mid_other_h)
    cp("out", mid_mine, mid_mine_h)
    cp("out", gdot, gdot_h)
    cp.finish()


def k_last(
    me, gat0, gat1, gat2, gat3, tab_h, perm_h, g_h, q_h, lam_h, nf_h, t_h, enter_h, pre_h, normed_h, gain_h, gdot_h, gpart_h, *rest
):
    pieces = rest[:8]
    bpi_h, bpf_h, small_h, mine_h, other_h = rest[8:13]
    (order, tab, perm, g, q, lam, nf, t, enter, pre, normed, gain, gdot, gpart, w, bpi, bpf, mine, other, lead, sums,
     small, sems) = rest[13:]
    cp = Copies(sems)
    summaries(cp, me, (gat0, gat1, gat2, gat3), order)
    cp("order", tab_h, tab)
    cp("order", perm_h, perm)
    cp("a", g_h, g)
    cp("a", q_h, q)
    cp("a", lam_h, lam)
    cp("a", nf_h, nf)
    cp("a", t_h, t)
    cp("a", enter_h, enter)
    cp("a", pre_h, pre)
    cp("b", normed_h, normed)
    cp("b", gain_h, gain)
    cp("b", gdot_h, gdot)
    cp("b", gpart_h, gpart)
    fetch_mix(cp, "b", pieces, (0, 3), w, 0)
    cp.wait("order")
    c512, s512 = row(tab, C512), row(tab, S512)
    c64, s64 = row(tab, C64), row(tab, S64)
    er = jnp.zeros((1, CH), F32)
    ei = jnp.zeros((1, CH), F32)
    for d in range(31, 0, -1):
        pd = row(order, 8 * d)
        nr = row(order, 8 * d + 1) + pd * (c512 * er + s512 * ei)
        ni = row(order, 8 * d + 2) + pd * (c512 * ei - s512 * er)
        er = jnp.where(d > me[0], nr, er)
        ei = jnp.where(d > me[0], ni, ei)
    sums[...] = jnp.zeros_like(sums)
    sums[0:1, :] = er
    sums[1:2, :] = ei
    back = exact_t(sums[0:SEG, :], perm[...])
    er = back[0:1, :]
    ei = back[1:2, :]
    cp.wait("a")
    for b in range(SEG - 1, -1, -1):
        lead[b : b + 1, :] = er
        lead[SEG + b : SEG + b + 1, :] = ei
        a0 = row(lam, b) * wide(row(nf, b))
        tr = a0 * (g[b : b + 1, 0:CH] + row(q, b) * er)
        ti = a0 * (g[b : b + 1, CH:] + row(q, b) * ei)
        er = c64 * tr + s64 * ti
        ei = c64 * ti - s64 * tr
    sums[...] = jnp.zeros_like(sums)

    def chunk(r, i, sr, si):
        ber = lead[0:SEG, :]
        bei = lead[SEG : 2 * SEG, :]
        ber = jnp.concatenate([ber, ber], axis=0)
        bei = jnp.concatenate([bei, bei], axis=0)
        qq = q[r, :]
        gr = g[r, 0:CH] + qq * ber
        gi = g[r, CH:] + qq * bei
        ct, st = turns(tab, i, 2)
        l = lam[r, :]
        keep_carry = wide(nf[r, :])
        adm = 1.0 - l
        xr = pre[r, 0:CH]
        xi = pre[r, CH:]
        zr = jax.nn.sigmoid(xr)
        zi = jax.nn.sigmoid(xi)
        ur = gr * ct - gi * st
        ui = gr * st + gi * ct
        dot_s = gr * sr + gi * si
        turn = gi * sr - gr * si
        back_lam = keep_carry * dot_s - (ur * (xr * zr) + ui * (xi * zi))
        bf = back_lam * l * adm
        bpf[r, :] = bf.astype(BF16)
        bpi[r, 0:CH] = (adm * ur * (zr * (1.0 + xr * (1.0 - zr)))).astype(BF16)
        bpi[r, CH:] = (adm * ui * (zi * (1.0 + xi * (1.0 - zi)))).astype(BF16)
        rot = l * keep_carry * turn
        sums[0:SEG, :] += bf[0:SEG, :] + bf[SEG : 2 * SEG, :]
        sums[SEG : 2 * SEG, :] += rot[0:SEG, :] + rot[SEG : 2 * SEG, :]

    chunk(
        pl.ds(0, 2 * SEG),
        0,
        jnp.concatenate([enter[0:SEG, :], t[0:SEG, 0:CH]], axis=0),
        jnp.concatenate([enter[SEG : 2 * SEG, :], t[0:SEG, CH:]], axis=0),
    )

    def step(r, i):
        before = pl.ds(pl.multiple_of(i * 16 - SEG, SEG), 16)
        chunk(r, i, t[before, 0:CH], t[before, CH:])

    loop(ROWS // 16, 16, step, 1)
    cp("out", bpi, bpi_h)
    cp("out", bpf, bpf_h)
    cp.wait("b")
    n = normed[...]
    dots = gdot[...]
    for i, left in enumerate((bpi[:, 0:CH], bpi[:, CH:], bpf[...])):
        grad = tn(left, n)
        put_grad(grad, i, mine, other)
        dots = dots + jnp.sum(grad * w[i].astype(F32), axis=0, keepdims=True)
    cp("out", other, other_h)
    cp("out", mine, mine_h)
    first = me[0] % 2 == 0
    small[...] = jnp.zeros_like(small)
    for i, part in enumerate((dots / gain[...], gpart[...])):
        own, rest_half = part[:, :H], part[:, H:]
        small[2 * i : 2 * i + 1, :] = jnp.where(first, own, rest_half)
        small[2 * i + 1 : 2 * i + 2, :] = jnp.where(first, rest_half, own)
    total_b = jnp.sum(sums[0:SEG, :], axis=0, keepdims=True)
    total_r = jnp.sum(sums[SEG : 2 * SEG, :], axis=0, keepdims=True)
    sums[...] = jnp.zeros_like(sums)
    sums[0:1, :] = total_b
    sums[1:2, :] = total_r
    small[4:6, :] = exact(sums[0:SEG, :], perm[...])[0:2]
    cp("out", small, small_h)
    cp.finish()


def k_input(x_h, keep_h, gain_h, bm_h, bpi_h, bpf_h, bpg_h, act_h, mixed_h, *rest):
    pieces, mlp_p = rest[:8], rest[8:16]
    grad_h, out_h, w, wd, x, keep, gain, bm, bpi, bpf, bpg, act, mixed, bn, grad, out, sems = rest[16:]
    cp = Copies(sems)
    cp("d", act_h, act)
    fetch_mlp(cp, "d", mlp_p, 2, wd, 0)
    cp("d", mixed_h, mixed)
    cp("a", bpi_h, bpi)
    fetch_mix(cp, "a", pieces, (0, 2), w, 0)
    cp("b", bpf_h, bpf)
    cp("b", bpg_h, bpg)
    fetch_mix(cp, "b", pieces, (2, 3), w, 2)
    cp("c", x_h, x)
    cp("c", keep_h, keep)
    cp("c", gain_h, gain)
    cp("c", bm_h, bm)
    cp.wait("d")
    out[...] = (mixed[...] + nn(act[...], wd[0])).astype(BF16)
    cp("out", out, out_h)
    cp.wait("a")
    bn[...] = nn(bpi[...], w[0:2].reshape(2 * CH, D))
    cp.wait("b")
    bn[...] += nn(bpf[...], w[2]) + nn(bpg[...], w[3:5].reshape(2 * CH, D))
    cp.wait("c")

    def norm(r, i):
        v = x[r, :].astype(F32)
        rs = lax.rsqrt(jnp.mean(v * v, axis=-1, keepdims=True) + EPS)
        u1 = bn[r, :] * gain[...] * keep[r, :1]
        m = jnp.mean(u1 * v, axis=-1, keepdims=True)
        grad[r, :] = (bm[r, :] + rs * u1 - v * (rs * rs * rs * m)).astype(BF16)

    loop(8, 64, norm)
    cp("out", grad, grad_h)
    cp.finish()


ANY = pl.BlockSpec(memory_space=pl.ANY)
SM = pl.BlockSpec(memory_space=pltpu.SMEM)


def call(kernel, args, outs, scratch, copies, scalar=True, vmem=60, us=5):
    specs = [ANY] * len(args)
    if scalar:
        specs[0] = SM
    return pl.pallas_call(
        kernel,
        in_specs=specs,
        out_specs=[ANY] * len(outs),
        out_shape=[jax.ShapeDtypeStruct(s, t) for s, t in outs],
        scratch_shapes=[pltpu.VMEM(s, t) for s, t in scratch] + [pltpu.SemaphoreType.DMA((copies,))],
        compiler_params=pltpu.CompilerParams(vmem_limit_bytes=vmem * 1024 * 1024),
        name=kernel.__name__,
        cost_estimate=pl.CostEstimate(flops=us, bytes_accessed=us, transcendentals=0),
    )(*args)


def device(z, y, c):
    return ((z % NZ) * NY + (y % NY)) * 2 + c


EVERY = [(z, y, c) for z in range(NZ) for y in range(NY) for c in range(2)]


def swap_core(v):
    return lax.ppermute(v, "ch", [(device(z, y, c), device(z, y, 1 - c)) for z, y, c in EVERY])


def move_z(v, k):
    return lax.ppermute(v, "ch", [(device(z, y, c), device(z + k, y, c)) for z, y, c in EVERY])


def move_y(v, k):
    return lax.ppermute(v, "ch", [(device(z, y, c), device(z, y + k, c)) for z, y, c in EVERY])


def move_x(v, k):
    return lax.ppermute(v, "dp", [(i, (i + k) % NX) for i in range(NX)])


def partner(i, c, k):
    return (i, i ^ 1, 3 - i, i ^ 2)[SWAP[k] if c else k]


def exchange_z(v, k):
    return lax.ppermute(v, "ch", [(device(z, y, c), device(partner(z, c, k), y, c)) for z, y, c in EVERY])


def exchange_y(v, k):
    return lax.ppermute(v, "ch", [(device(z, y, c), device(z, partner(y, c, k), c)) for z, y, c in EVERY])


def exchange_x(v, k):
    return lax.ppermute(
        v,
        ("dp", "ch"),
        [(x * 32 + device(z, y, c), partner(x, c, k) * 32 + device(z, y, c)) for x in range(NX) for z, y, c in EVERY],
    )


def after(value, *others):
    return lax.optimization_barrier((value,) + others)[0]


def gather_chip(mine, other, rows, core):
    got = swap_core(other)[:, :rows]
    mine = mine[:, :rows]
    return jnp.where(
        core == 0, jnp.concatenate([mine, got], axis=1), jnp.concatenate([got, mine], axis=1)
    )


def gather_line(v, move):
    return [v] + [move(v, -k) for k in (1, 2, 3)]


def gather_ring(v, exchange, earlier=None):
    one, two = exchange(v, 1), exchange(v, 2)
    if earlier is not None:
        one, two = lax.optimization_barrier((one, two) + earlier)[:2]
    return [v, one, two, exchange(one, 2)]


def summary_pair(summary):
    return jnp.concatenate([summary, swap_core(summary)], axis=0)


def summary_line(pair):
    return jnp.concatenate(gather_line(pair, move_z), axis=0)


def add4(own, near, far, near_too):
    a, b, c, d = [v.astype(F32) for v in (own, near, far, near_too)]
    return (a + c) + (b + d)


def reduce_core(mine, other):
    return (mine.astype(F32) + swap_core(other).astype(F32)).astype(BF16)


def reduce_pieces(pieces, move):
    return add4(pieces[0], *[move(pieces[k], k) for k in (1, 2, 3)])


def reduce_outer(pieces, exchange):
    return add4(pieces[0], *[exchange(pieces[k], k) for k in (1, 3, 2)])


def reduce_half(slots, exchange):
    return (slots[:2].astype(F32) + exchange(slots[2:], 1).astype(F32)).astype(BF16)


def reduce_last(two, exchange):
    return two[0].astype(F32) + exchange(two[1], 2).astype(F32)


def reduce_four(pieces, exchange):
    slots = jnp.stack([pieces[0], pieces[2], pieces[1], pieces[3]])
    return reduce_last(reduce_half(slots, exchange), exchange).astype(BF16)


def finish(keep, send, core):
    got = swap_core(send)
    return jnp.where(
        core == 0, jnp.concatenate([keep, got], axis=-1), jnp.concatenate([got, keep], axis=-1)
    )


def finish_units(own, core):
    keep = jnp.where(core == 0, own[:, :12], own[:, 12:])
    send = jnp.where(core == 0, own[:, 12:], own[:, :12])
    return finish(keep, send, core)


def finish_mlp(chip, core, xi):
    groups = gather_line(chip, move_x)

    def of_plane(g):
        k = (g + NX - xi) % NX
        return jnp.where(k < 2, jnp.where(k == 0, groups[0], groups[1]), jnp.where(k == 2, groups[2], groups[3]))

    kinds = jnp.stack([of_plane(g) for g in range(NX)]).reshape(3, 2, 48, H)
    keep = jnp.where(core == 0, kinds[:, 0], kinds[:, 1])
    send = jnp.where(core == 0, kinds[:, 1], kinds[:, 0])
    return finish(keep, send, core).astype(F32)


def halves(rows):
    hi = lax.reduce_precision(rows, 8, 7)
    return jnp.concatenate([hi, lax.reduce_precision(rows - hi, 8, 7)], axis=0).astype(BF16)


def end_phase(pieces, small, move, reduce):
    units, rows = pieces[0].shape[0], pieces[0].shape[0] * pieces[0].shape[1]
    tail = halves(small)
    total = reduce([jnp.concatenate([p.reshape(rows, H), tail], axis=0) for p in pieces], move)
    return total[:rows].astype(BF16).reshape(units, -1, H), total[rows : rows + 8] + total[rows + 8 :]


def to_steps(v):
    return v.reshape(SEG, STEPS, *v.shape[1:]).swapaxes(0, 1).reshape(v.shape)


def from_steps(v):
    return v.reshape(STEPS, SEG, *v.shape[1:]).swapaxes(0, 1).reshape(v.shape)


def shards(
    block_input, gain_mix, w_input, w_forget, w_outgate, bias_forget, rotation, w_out,
    gain_mlp, w_gate, w_up, w_down, seq_lengths, pad_mask, cotangent,
):
    place = lax.axis_index("ch").astype(jnp.int32)
    xi = lax.axis_index("dp").astype(jnp.int32)
    core = place % 2
    y = (place // 2) % NY
    z = place // (2 * NY)

    def own_first(v):
        return jnp.where(core == 0, v, jnp.concatenate([v[..., H:], v[..., :H]], axis=-1))

    vec = jnp.concatenate([bias_forget, rotation])
    hi = lax.reduce_precision(vec, 8, 7)
    mid = lax.reduce_precision(vec - hi, 8, 7)
    extra = jnp.concatenate([hi, mid, vec - hi - mid]).astype(BF16)
    me = jnp.stack([place, xi])
    mix_mine, mix_other, mlp_mine, mlp_other = call(
        k_pack,
        [me, w_input.T, w_forget.T, w_outgate.T, w_out, w_gate.T, w_up.T, w_down],
        [((MIX_U, 16, H), BF16)] * 2 + [((3, 48, H), BF16)] * 2,
        [((24, D), BF16), ((12, D), BF16), ((24, D), BF16), ((24, D), BF16), ((3, 48, D), BF16)]
        + [((MIX_U, 16, H), BF16)] * 2 + [((3, 48, H), BF16)] * 2,
        11,
    )
    rows = MIX_U * UNIT
    mix_chip = gather_chip(mix_mine, mix_other, 12, core).reshape(rows, H)
    mix_chip = jnp.concatenate([mix_chip, jnp.pad(extra[None], ((0, 7), (0, H - 72)))], axis=0)
    mlp_chip = gather_chip(mlp_mine, mlp_other, 48, core)
    mix_line = gather_line(mix_chip, move_y)
    mlp_line = gather_line(mlp_chip, move_z)
    mix_line, block_input, cotangent, seq_lengths, pad_mask = lax.optimization_barrier(
        (mix_line, block_input, cotangent, seq_lengths, pad_mask)
    )
    mix_line = jnp.concatenate(
        [jnp.concatenate([f[:rows].reshape(MIX_U, UNIT, H) for f in mix_line], axis=1).reshape(VEC, H)]
        + [f[rows:] for f in mix_line],
        axis=0,
    )
    j = jnp.arange(CH, dtype=jnp.int32)
    rest = j % 96
    ky, tail = rest // UNIT, rest % UNIT
    flip = jnp.where(core == 0, jnp.array([0, 1, 3, 2]), jnp.array([0, 3, 1, 2])).astype(jnp.int32)
    where_to = jnp.bitwise_xor(jnp.repeat(flip, 96), z) * 96 + ((ky + y) % NY) * UNIT + tail
    perm = (where_to[:, None] == j[None, :]).astype(F32)

    lengths = seq_lengths[0]
    ends = jnp.sum(jnp.where(jnp.arange(8)[:, None] >= jnp.arange(8)[None, :], lengths[None, :], 0), axis=1)
    starts = ends - lengths
    r = jnp.arange(ROWS, dtype=jnp.int32)
    position = place * ROWS + (r % SEG) * STEPS + r // SEG
    first = jnp.any(position[:, None] == starts[None, :], axis=1)
    nf = jnp.broadcast_to(1.0 - first.astype(F32)[:, None], (ROWS, 128))
    keep = jnp.broadcast_to(to_steps(pad_mask.astype(F32))[:, None], (ROWS, 128))

    x = own_first(to_steps(block_input))
    ups = own_first(to_steps(cotangent)) * keep[:, :1].astype(BF16)
    gain1 = own_first(gain_mix)[None]
    gain2 = own_first(gain_mlp)[None]
    number = jnp.where(core == 0, jnp.array([0, 1, 3, 2]), jnp.array([0, 2, 3, 1])).astype(jnp.int32)
    number = [jnp.take(number, jnp.bitwise_xor(xi, g)) for g in range(NX)]
    slot = [jnp.where((k == 1) | (k == 2), 3 - k, k) for k in number]
    me = jnp.stack([place, xi] + slot + number)

    wide_f = ((ROWS, D), F32)
    wide_b = ((ROWS, D), BF16)
    half_f = ((ROWS, CH), F32)
    half_b = ((ROWS, CH), BF16)
    lanes = ((ROWS, 128), F32)
    tab_s = ((TAB, CH), F32)
    perm_s = ((CH, CH), F32)
    few = ((SEG, CH), F32)
    pair = ((2 * SEG, CH), F32)
    gain_s = ((1, D), F32)
    order_s = ((32 * SEG, CH), F32)

    (normed,) = call(
        k_norm, [x, keep, gain1], [wide_b], [wide_b, lanes, gain_s, wide_b], 4, scalar=False, us=3
    )
    mix_own = gather_ring(mix_line, exchange_z, (normed, ups, nf, perm))
    mlp_own = gather_ring(jnp.concatenate(mlp_line, axis=1), exchange_y, (mix_own[3],))
    mix_own[0] = after(mix_own[0], mix_own[1])
    mix_w = mix_own + [swap_core(p) for p in mix_own]
    mlp_early = [swap_core(after(mlp_own[0], mix_own[1])), swap_core(mlp_own[1])]
    nf, mlp_early = lax.optimization_barrier((nf, mlp_early))
    pre, s, lam, cum, tab, summary = call(
        k_project,
        [me, normed, nf, perm] + mix_w,
        [wide_f, wide_f, half_f, half_f, tab_s, few],
        [((3, CH, D), BF16), wide_b, lanes, perm_s, ((256, H), BF16), wide_f, half_f, wide_f, half_f, half_f, tab_s,
         few],
        44,
        us=6,
    )
    line, mlp_own = lax.optimization_barrier((summary_line(summary_pair(summary)), mlp_own))
    before = gather_line(line, move_y)
    mlp_w = mlp_own + mlp_early + [swap_core(p) for p in mlp_own[2:]]
    hidden = ((ROWS, FF), BF16)
    mlp_g = ((4, 3, 4 * 96, H), BF16)
    mlp_s = ((12, 4 * 96, H), BF16)
    mid_g = ((4, 4, 96, H), BF16)
    (t, enter, act, mixed, bm, g, q, bpg, gpart, gdot, summary_back, mlp_mine, mlp_other, mid_mine, mid_other) = call(
        k_middle,
        [me] + before + [tab, perm, s, cum, normed, x, gain2, ups, lam, nf] + mix_w + mlp_w,
        [wide_f, pair, hidden, wide_f, wide_f, wide_f, half_f, wide_b, gain_s, gain_s, few, mlp_g, mlp_g, mid_g, mid_g],
        [((2, CH, D), BF16), ((2, CH, D), BF16), ((3, FF, D), BF16), order_s, tab_s, perm_s, wide_f, half_f, wide_b,
         wide_b, gain_s, wide_b, half_f, lanes, few, pair, wide_f, wide_b, wide_f, wide_b, hidden, hidden, hidden, mlp_s,
         mlp_s, wide_f, wide_b, wide_f, half_f, wide_b, gain_s, gain_s, mid_g, mid_g],
        150,
        vmem=62,
        us=20,
    )
    mlp_send = reduce_core(mlp_mine[2:], mlp_other[2:])
    line = summary_line(after(summary_pair(summary_back), mlp_send))
    mlp_keep = reduce_core(mlp_mine[:2], mlp_other[:2])
    mid_both = after(reduce_core(mid_mine, mid_other), line)
    behind = gather_line(line, move_y)
    mlp_two = (mlp_keep.astype(F32) + exchange_x(mlp_send, 1).astype(F32)).astype(BF16)
    behind[0] = after(behind[0], mlp_two)
    end_g = ((4, 3, 96, H), BF16)
    bpi, bpf, small, end_mine, end_other = call(
        k_last,
        [me] + behind + [tab, perm, g, q, lam, nf, t, enter, pre, normed, gain1, gdot, gpart] + mix_w,
        [wide_b, half_b, few, end_g, end_g],
        [order_s, tab_s, perm_s, wide_f, half_f, half_f, lanes, wide_f, pair, wide_f, wide_b, gain_s, gain_s, gain_s,
         ((3, CH, D), BF16), wide_b, half_b, end_g, end_g, pair, pair, few],
        80,
        us=6,
    )
    end_both = reduce_core(end_mine, end_other)
    small = small + swap_core(small)
    bpi, end_both, small = lax.optimization_barrier((bpi, end_both, small))
    grad_input, out = call(
        k_input,
        [x, keep, gain1, bm, bpi, bpf, bpg, act, mixed] + mix_w + mlp_w,
        [wide_b, wide_b],
        [((5, CH, D), BF16), ((1, FF, D), BF16), wide_b, lanes, gain_s, wide_f, wide_b, half_b, wide_b, hidden, wide_f,
         wide_f, wide_b, wide_b],
        70,
        scalar=False,
        us=5,
    )
    mid_line = reduce_four([mid_both[k] for k in range(4)], exchange_z)
    end_line, small = end_phase([end_both[k] for k in range(4)], small, exchange_z, reduce_outer)
    end_line, grad_input, out = lax.optimization_barrier((end_line, grad_input, out))
    line = jnp.concatenate([end_line, mid_line], axis=0).reshape(MIX_U, 4, UNIT, H)
    own, small = end_phase([line[:, k] for k in range(4)], small, move_y, reduce_pieces)
    own = jnp.concatenate([own.reshape(MIX_U * UNIT, H), halves(small)], axis=0)
    total = reduce_pieces([own] * 4, move_x)
    grads_mix = finish_units(total[: MIX_U * UNIT].reshape(MIX_U, UNIT, H), core)
    small = total[MIX_U * UNIT : MIX_U * UNIT + 8] + total[MIX_U * UNIT + 8 :]

    mlp_got = after(exchange_x(mlp_two[1], 2), grad_input)
    mlp_own = (mlp_two[0].astype(F32) + mlp_got.astype(F32)).astype(BF16).reshape(3, 4, 96, H)
    mlp_line = reduce_outer([mlp_own[:, k] for k in range(4)], exchange_y).astype(BF16).reshape(3, 4, UNIT, H)
    mlp_chip = reduce_pieces([mlp_line[:, k] for k in range(4)], move_z).astype(BF16)
    grads_mlp = finish_mlp(mlp_chip, core, xi)
    bias_grad = lax.dynamic_slice(small[4], (place * 12,), (12,))
    rot_grad = lax.dynamic_slice(small[5], (place * 12,), (12,))

    def together(re_im):
        return re_im.swapaxes(0, 1).reshape(UNIT, D)

    return (
        from_steps(own_first(out)),
        from_steps(own_first(grad_input)),
        small[0:2].reshape(D),
        together(grads_mix[0:2]).T,
        grads_mix[2].T,
        together(grads_mix[3:5]).T,
        bias_grad,
        rot_grad,
        together(grads_mix[5:7]),
        small[2:4].reshape(D),
        grads_mlp[0].T,
        grads_mlp[1].T,
        grads_mlp[2],
    )


def solution(mesh):
    rows = P(("dp", "ch"), None)
    cols = P(None, "ch")
    return jax.shard_map(
        shards,
        mesh=mesh,
        in_specs=(
            rows, P(), cols, cols, cols, P("ch"), P("ch"), P("ch", None), P(), cols, cols,
            P("ch", None), P("dp", None), P(("dp", "ch")), rows,
        ),
        out_specs=(
            rows, rows, P(), cols, cols, cols, P("ch"), P("ch"), P("ch", None), P(), cols, cols,
            P("ch", None),
        ),
        check_vma=False,
    )
```

```python
import jax
import jax.numpy as jnp
from jax import lax
from jax.experimental import pallas as pl
from jax.experimental.pallas import tpu as pltpu
from jax.sharding import PartitionSpec as P

EPS = 1e-06
F32 = jnp.float32
BF16 = jnp.bfloat16

ROWS = 512
D = 768
H = 384
CH = 384
FF = 1536
SEG = 8
STEPS = ROWS // SEG
NZ, NY, NX = 4, 4, 4
UNIT = 24
MIX_U = 7
VEC = 96 * MIX_U
COS, SIN, C64, S64, C512, S512, BIAS = 0, 64, 128, 129, 130, 131, 132
TAB = 136
SWAP = (0, 2, 1, 3)


def nt(a, b):
    return lax.dot_general(a, b, (((1,), (1,)), ((), ())), preferred_element_type=F32)


def nn(a, b):
    return lax.dot_general(a, b, (((1,), (0,)), ((), ())), preferred_element_type=F32)


def tn(a, b):
    return lax.dot_general(a, b, (((0,), (0,)), ((), ())), preferred_element_type=F32)


def exact(a, b):
    return lax.dot_general(
        a, b, (((1,), (0,)), ((), ())), precision=lax.Precision.HIGHEST, preferred_element_type=F32
    )


def exact_t(a, b):
    return lax.dot_general(
        a, b, (((1,), (1,)), ((), ())), precision=lax.Precision.HIGHEST, preferred_element_type=F32
    )


def wide(col):
    return jnp.concatenate([col, col, col], axis=1)


def loop(count, size, body, start=0, unroll=2):
    def step(i, _):
        body(pl.ds(pl.multiple_of(i * size, size), size), i)
        return 0

    lax.fori_loop(start, count, step, 0, unroll=unroll)


class Copies:
    def __init__(self, sems):
        self.sems = sems
        self.used = 0
        self.open = {}

    def __call__(self, name, src, dst):
        copy = pltpu.make_async_copy(src, dst, self.sems.at[self.used])
        self.used += 1
        copy.start()
        self.open.setdefault(name, []).append(copy)

    def wait(self, *names):
        for name in names:
            for copy in self.open.pop(name):
                copy.wait()

    def finish(self):
        self.wait(*list(self.open))


def fetch_mix(cp, name, pieces, units, scratch, at):
    for u in range(units[0], units[0] + units[1]):
        for half in range(2):
            for k in range(4):
                cp(
                    name,
                    pieces[half * 4 + (SWAP[k] if half else k)].at[pl.ds(96 * u, 96)],
                    scratch.at[at + u - units[0], pl.ds(96 * k, 96), pl.ds(H * half, H)],
                )


def fetch_mlp(cp, name, pieces, kind, scratch, at=None):
    for half in range(2):
        for k in range(4):
            cp(
                name,
                pieces[half * 4 + (SWAP[k] if half else k)].at[kind],
                scratch.at[kind if at is None else at, pl.ds(CH * k, CH), pl.ds(H * half, H)],
            )


def put_grad(grad, unit, mine, other):
    low = grad.astype(BF16)
    for k in range(4):
        mine[k, unit] = low[96 * k : 96 * k + 96, :H]
        other[SWAP[k], unit] = low[96 * k : 96 * k + 96, H:]


def turns(tab, i, steps):
    rows = []
    for base in (COS, SIN):
        parts = [
            jnp.broadcast_to(tab[pl.ds(base + i * steps + s, 1), :], (SEG, CH)) for s in range(steps)
        ]
        rows.append(parts[0] if steps == 1 else jnp.concatenate(parts, axis=0))
    return rows


def row(ref, i):
    return ref[i : i + 1, :]


def summaries(cp, me, pieces, order):
    y = (me[0] // 2) % NY
    z = me[0] // (2 * NY)
    for kz in range(NZ):
        for ky in range(NY):
            chip = ((z + kz) % NZ) * NY + (y + ky) % NY
            cp(
                "order",
                pieces[ky].at[pl.ds(kz * SEG, SEG)],
                order.at[pl.ds(pl.multiple_of(chip * SEG, SEG), SEG)],
            )


def summary_of(order, me, d):
    tile = order[d // 2 * SEG : d // 2 * SEG + SEG, :]
    rows = jnp.where(me[0] % 2 == d % 2, tile[0:3], tile[3:6])
    return rows[0:1], rows[1:2], rows[2:3]


def put_summary(pt, er, ei, sums, perm):
    sums[...] = jnp.zeros_like(sums)
    for at in (0, SEG + 3):
        sums[at : at + 1, :] = pt
        sums[at + 1 : at + 2, :] = er
        sums[at + 2 : at + 3, :] = ei
    sums[...] = exact(sums[...], perm[...])


def numbers(me, g):
    apart = lax.bitwise_xor(me[1], g)
    same = jnp.where(me[0] % 2 == 0, 1, 3)
    own = jnp.where(apart == 0, 0, jnp.where(apart == 2, 3, jnp.where(apart == same, 1, 2)))
    return own, jnp.where((own == 1) | (own == 2), 3 - own, own)


def k_pack(me, in_h, forget_h, gate_h, out_h, ffn_gate_h, ffn_up_h, ffn_down_h, mix_mine_h, mix_other_h, mlp_mine_h, mlp_other_h, *rest):
    w_in, w_forget, w_gate, w_out, w, mix_mine, mix_other, mlp_mine, mlp_other, sems = rest
    cp = Copies(sems)
    cp("mix", in_h, w_in)
    cp("mix", forget_h, w_forget)
    cp("mix", gate_h, w_gate)
    cp("mix", out_h, w_out)
    for i, ref in enumerate((ffn_gate_h, ffn_up_h, ffn_down_h)):
        cp("mlp", ref, w.at[i])
    first = me[0] % 2 == 0

    def put(value, mine, other):
        left, right = value[:, :H], value[:, H:]
        mine[...] = jnp.where(first, left, right).astype(BF16)
        other[...] = jnp.where(first, right, left).astype(BF16)

    def pick(columns, factor, offset):
        at = lax.broadcasted_iota(jnp.int32, (16, columns), 0) * factor + offset
        return jnp.where(at == lax.broadcasted_iota(jnp.int32, (16, columns), 1), 1.0, 0.0).astype(BF16)

    every_other = (pick(24, 2, 0), pick(24, 2, 1))
    each = pick(12, 1, 0)
    cp.wait("mix")
    for unit, ref in ((0, w_in), (3, w_gate), (5, w_out)):
        for part in range(2):
            put(nn(every_other[part], ref[...]), mix_mine.at[unit + part], mix_other.at[unit + part])
    put(nn(each, w_forget[...]), mix_mine.at[2], mix_other.at[2])
    cp("out", mix_other, mix_other_h)
    cp("out", mix_mine, mix_mine_h)
    cp.wait("mlp")
    for i in range(3):
        put(w[i].astype(F32), mlp_mine.at[i], mlp_other.at[i])
    cp("out", mlp_other, mlp_other_h)
    cp("out", mlp_mine, mlp_mine_h)
    cp.finish()


def k_norm(x_h, keep_h, gain_h, normed_h, x, keep, gain, normed, sems):
    cp = Copies(sems)
    cp("x", x_h, x)
    cp("x", keep_h, keep)
    cp("x", gain_h, gain)
    cp.wait("x")

    def norm(r, i):
        v = x[r, :].astype(F32)
        rs = lax.rsqrt(jnp.mean(v * v, axis=-1, keepdims=True) + EPS) * keep[r, :1]
        normed[r, :] = (v * rs * gain[...]).astype(BF16)

    loop(8, 64, norm)
    cp("out", normed, normed_h)
    cp.finish()


def k_project(me, normed_h, nf_h, perm_h, *rest):
    pieces = rest[:8]
    pre_h, s_h, lam_h, cum_h, tab_h, summary_h, summary2_h = rest[8:15]
    w, normed, nf, perm, vecs, pre, pf, s, lam, cum, tab, sums, sems = rest[15:]
    cp = Copies(sems)
    for i in range(8):
        cp("vecs", pieces[i].at[pl.ds(VEC, 32)], vecs.at[pl.ds(32 * i, 32)])
    cp("w", normed_h, normed)
    fetch_mix(cp, "w", pieces, (0, 3), w, 0)
    cp("nf", perm_h, perm)
    cp("nf", nf_h, nf)

    cp.wait("vecs")
    group = lax.broadcasted_iota(jnp.int32, (32, 256), 0)
    half = (group + me[0]) % 2
    kz = group // 8
    kz = jnp.where((half == 1) & (kz > 0) & (kz < 3), 3 - kz, kz)
    source = 32 * (half * 4 + kz) + 8 * ((group // 2) % 4)
    choose = jnp.where(source == lax.broadcasted_iota(jnp.int32, (32, 256), 1), 1.0, 0.0).astype(BF16)
    values = nn(choose, vecs[...])[:, :128].astype(BF16)
    sub = lax.broadcasted_iota(jnp.int32, (128, CH), 0)
    same = (sub % 12 == lax.broadcasted_iota(jnp.int32, (128, CH), 1) % 12) & (sub < 72)
    hit = lax.broadcasted_iota(jnp.int32, (32, CH), 0) == lax.broadcasted_iota(jnp.int32, (32, CH), 1) // 12
    found = []
    for v in range(2):
        pick = jnp.where(same & ((sub % 24) // 12 == v), 1.0, 0.0).astype(BF16)
        found.append(jnp.sum(jnp.where(hit, nn(values, pick), 0.0), axis=0, keepdims=True))
    bias, rot = found
    few = lax.broadcasted_iota(jnp.int32, (SEG, CH), 0)
    one = few.astype(F32) * rot
    eight = one * 8.0
    far = jnp.where(few < 2, float(STEPS), float(ROWS)) * rot
    c_one, s_one, c_eight, s_eight = jnp.cos(one), jnp.sin(one), jnp.cos(eight), jnp.sin(eight)
    for i in range(SEG):
        ca, sa = c_eight[i : i + 1], s_eight[i : i + 1]
        tab[COS + SEG * i : COS + SEG * i + SEG, :] = ca * c_one - sa * s_one
        tab[SIN + SEG * i : SIN + SEG * i + SEG, :] = sa * c_one + ca * s_one
    cos, sin = jnp.cos(far), jnp.sin(far)
    c64, s64 = cos[0:1], sin[0:1]
    cp.wait("nf")
    far = exact(jnp.where(few % 2 == 0, cos, sin), perm[...])
    tab[C64:TAB, :] = jnp.zeros((SEG, CH), F32)
    tab[C64 : C64 + 1, :] = c64
    tab[S64 : S64 + 1, :] = s64
    tab[C512 : C512 + 1, :] = far[2:3]
    tab[S512 : S512 + 1, :] = far[3:4]
    cp("out", tab, tab_h)

    cp.wait("w")
    n = normed[...]
    pre[...] = nt(n, w[0:2].reshape(2 * CH, D))
    pf[...] = nt(n, w[2])
    cp("out", pre, pre_h)

    def step(t, carry):
        sr, si, p = carry
        r = pl.ds(pl.multiple_of(t * SEG, SEG), SEG)
        l = jax.nn.sigmoid(pf[r, :] + bias)
        a = l * wide(nf[r, :])
        adm = 1.0 - l
        vr = pre[r, 0:CH]
        vi = pre[r, CH:]
        vr = adm * vr * jax.nn.sigmoid(vr)
        vi = adm * vi * jax.nn.sigmoid(vi)
        ct, st = turns(tab, t, 1)
        sr = a * sr + (vr * ct + vi * st)
        si = a * si + (vi * ct - vr * st)
        p = a * p
        lam[r, :] = l
        s[r, 0:CH] = sr
        s[r, CH:] = si
        cum[r, :] = p
        return sr, si, p

    zero = jnp.zeros((SEG, CH), F32)
    sr, si, p = lax.fori_loop(0, STEPS, step, (zero, zero, zero + 1.0), unroll=8)
    cp("out", s, s_h)
    cp("out", lam, lam_h)
    cp("out", cum, cum_h)
    er = jnp.zeros((1, CH), F32)
    ei = jnp.zeros((1, CH), F32)
    pt = jnp.ones((1, CH), F32)
    for b in range(SEG):
        pb = p[b : b + 1]
        tr = sr[b : b + 1] + pb * er
        ti = si[b : b + 1] + pb * ei
        er = c64 * tr - s64 * ti
        ei = c64 * ti + s64 * tr
        pt = pt * pb
    put_summary(pt, er, ei, sums, perm)
    cp("out", sums.at[pl.ds(0, SEG)], summary_h)
    cp("out", sums.at[pl.ds(SEG, SEG)], summary2_h)
    cp.finish()


def k_middle(
    me, gat0, gat1, gat2, gat3, tab_h, perm_h, s_h, cum_h, normed_h, x_h, gain_h, ups_h, lam_h, nf_h, *rest
):
    mix_p, mlp_p = rest[:8], rest[8:16]
    (t_h, enter_h, out_h, bm_h, g_h, q_h, bpg_h, gpart_h, gdot_h, summary_h, summary2_h, mine_h, other_h,
     mid_mine_h, mid_other_h) = rest[16:31]
    (wg, wo, w, order, tab, perm, s, cum, normed, x, gain, ups, lam, nf, sums, enter, pg, gated, mixed, nm, act, bg, bu,
     mine, other, bm, bml, g, q, bpg, gsum, gdot, mid_mine, mid_other, sems) = rest[31:]
    cp = Copies(sems)
    cp("gate", normed_h, normed)
    fetch_mix(cp, "gate", mix_p, (3, 2), wg, 0)
    summaries(cp, me, (gat0, gat1, gat2, gat3), order)
    cp("order", tab_h, tab)
    cp("order", perm_h, perm)
    cp("s", s_h, s)
    cp("s", cum_h, cum)
    fetch_mix(cp, "wo", mix_p, (5, 2), wo, 0)
    cp("x", x_h, x)
    cp("x", gain_h, gain)
    fetch_mlp(cp, "w_gate", mlp_p, 0, w)
    fetch_mlp(cp, "w_up", mlp_p, 1, w)
    cp("ups", ups_h, ups)
    fetch_mlp(cp, "w_down", mlp_p, 2, w)
    cp("lam", lam_h, lam)
    cp("lam", nf_h, nf)

    cp.wait("order", "gate")
    pg[...] = nt(normed[...], wg[...].reshape(2 * CH, D))
    c512, s512 = row(tab, C512), row(tab, S512)
    c64, s64 = row(tab, C64), row(tab, S64)
    er = jnp.zeros((1, CH), F32)
    ei = jnp.zeros((1, CH), F32)
    for d in range(31):
        pd, sr, si = summary_of(order, me, d)
        nr = sr + pd * (c512 * er - s512 * ei)
        ni = si + pd * (c512 * ei + s512 * er)
        er = jnp.where(d < me[0], nr, er)
        ei = jnp.where(d < me[0], ni, ei)
    sums[...] = jnp.zeros_like(sums)
    sums[0:1, :] = er
    sums[1:2, :] = ei
    back = exact_t(sums[0:SEG, :], perm[...])
    er = back[0:1, :]
    ei = back[1:2, :]
    cp.wait("s")
    last = ROWS - SEG
    for b in range(SEG):
        enter[b : b + 1, :] = er
        enter[SEG + b : SEG + b + 1, :] = ei
        pb = row(cum, last + b)
        tr = s[last + b : last + b + 1, 0:CH] + pb * er
        ti = s[last + b : last + b + 1, CH:] + pb * ei
        er = c64 * tr - s64 * ti
        ei = c64 * ti + s64 * tr
    cp("out", enter, enter_h)

    def fix(r, i):
        ber = enter[0:SEG, :]
        bei = enter[SEG : 2 * SEG, :]
        ber = jnp.concatenate([ber, ber], axis=0)
        bei = jnp.concatenate([bei, bei], axis=0)
        p = cum[r, :]
        sr = s[r, 0:CH] + p * ber
        si = s[r, CH:] + p * bei
        s[r, 0:CH] = sr
        s[r, CH:] = si
        ct, st = turns(tab, i, 2)
        gr = jax.nn.sigmoid(pg[r, 0:CH])
        gi = jax.nn.sigmoid(pg[r, CH:])
        pg[r, 0:CH] = gr
        pg[r, CH:] = gi
        gated[r, 0:CH] = ((sr * ct - si * st) * gr).astype(BF16)
        gated[r, CH:] = ((sr * st + si * ct) * gi).astype(BF16)

    loop(32, 16, fix)
    cp("out", s, t_h)
    cp.wait("wo")
    mixed[...] = nn(gated[...], wo[...].reshape(2 * CH, D))
    cp.wait("x")

    def norm(r, i):
        v = mixed[r, :] + x[r, :].astype(F32)
        mixed[r, :] = v
        rs = lax.rsqrt(jnp.mean(v * v, axis=-1, keepdims=True) + EPS)
        nm[r, :] = (v * rs * gain[...]).astype(BF16)

    loop(8, 64, norm)
    n = nm[...]
    cp.wait("w_gate", "w_up", "ups", "w_down")
    up_low = ups[...]
    for k in range(FF // 256):
        cols = slice(256 * k, 256 * k + 256)
        gp = nt(n, w[0, cols, :])
        up = nt(n, w[1, cols, :])
        ba = nt(up_low, w[2, cols, :])
        sg = jax.nn.sigmoid(gp)
        ga = gp * sg
        act[:, cols] = (ga * up).astype(BF16)
        bg[:, cols] = (ba * up * sg * (1.0 + gp * (1.0 - sg))).astype(BF16)
        bu[:, cols] = (ba * ga).astype(BF16)
    for kind, (left, right) in enumerate(((bg, n), (bu, n), (act, up_low))):
        for k in range(4):
            grad = tn(left[:, CH * k : CH * k + CH], right)
            for j in range(4):
                part = jnp.concatenate(
                    [grad[96 * i + UNIT * j : 96 * i + UNIT * j + UNIT] for i in range(4)], axis=0
                ).astype(BF16)
                mine[kind * 4 + j, 96 * k : 96 * k + 96, :] = part[:, :H]
                other[kind * 4 + j, 96 * SWAP[k] : 96 * SWAP[k] + 96, :] = part[:, H:]
        for j in range(4):
            unit = kind * 4 + j
            for_other, slot = numbers(me, unit // 3)
            cp("out", other.at[unit], other_h.at[for_other, unit % 3])
            cp("out", mine.at[unit], mine_h.at[slot, unit % 3])
    nm[...] = (mixed[...] + nn(act[...], w[2])).astype(BF16)
    cp("out", nm, out_h)
    bm[...] = nn(bg[...], w[0]) + nn(bu[...], w[1])
    gsum[...] = jnp.zeros_like(gsum)

    def norm_back(r, i):
        v = mixed[r, :]
        b = bm[r, :]
        rs = lax.rsqrt(jnp.mean(v * v, axis=-1, keepdims=True) + EPS)
        gsum[...] += jnp.sum(b * v * rs, axis=0, keepdims=True)
        u2 = b * gain[...]
        m = jnp.mean(u2 * v, axis=-1, keepdims=True)
        o = ups[r, :].astype(F32) + rs * u2 - v * (rs * rs * rs * m)
        bm[r, :] = o
        bml[r, :] = o.astype(BF16)

    loop(8, 64, norm_back)
    cp("out", bm, bm_h)
    cp("out", gsum, gpart_h)
    b = bml[...]
    g[...] = nt(b, wo[...].reshape(2 * CH, D))

    def gate(r, i):
        sr = s[r, 0:CH]
        si = s[r, CH:]
        ct, st = turns(tab, i, 2)
        gr = pg[r, 0:CH]
        gi = pg[r, CH:]
        br = g[r, 0:CH] * gr
        bi = g[r, CH:] * gi
        bpg[r, 0:CH] = (br * (sr * ct - si * st) * (1.0 - gr)).astype(BF16)
        bpg[r, CH:] = (bi * (sr * st + si * ct) * (1.0 - gi)).astype(BF16)
        g[r, 0:CH] = br * ct + bi * st
        g[r, CH:] = bi * ct - br * st

    loop(32, 16, gate)
    cp("out", bpg, bpg_h)
    cp.wait("lam")

    def step(i, carry):
        cr, ci, p = carry
        r = pl.ds(pl.multiple_of((STEPS - 1 - i) * SEG, SEG), SEG)
        a = lam[r, :] * wide(nf[r, :])
        gr = g[r, 0:CH] + cr
        gi = g[r, CH:] + ci
        g[r, 0:CH] = gr
        g[r, CH:] = gi
        q[r, :] = p
        return a * gr, a * gi, a * p

    zero = jnp.zeros((SEG, CH), F32)
    cr, ci, p = lax.fori_loop(0, STEPS, step, (zero, zero, zero + 1.0), unroll=8)
    cp("out", g, g_h)
    cp("out", q, q_h)
    er = jnp.zeros((1, CH), F32)
    ei = jnp.zeros((1, CH), F32)
    pt = jnp.ones((1, CH), F32)
    for i in range(SEG - 1, -1, -1):
        pb = p[i : i + 1, :]
        tr = cr[i : i + 1, :] + pb * er
        ti = ci[i : i + 1, :] + pb * ei
        er = c64 * tr + s64 * ti
        ei = c64 * ti - s64 * tr
        pt = pt * pb
    put_summary(pt, er, ei, sums, perm)
    cp("out", sums.at[pl.ds(0, SEG)], summary_h)
    cp("out", sums.at[pl.ds(SEG, SEG)], summary2_h)

    grad = tn(gated[...], bml[...])
    put_grad(grad[:CH], 2, mid_mine, mid_other)
    put_grad(grad[CH:], 3, mid_mine, mid_other)
    grad = tn(bpg[...], normed[...])
    put_grad(grad[:CH], 0, mid_mine, mid_other)
    put_grad(grad[CH:], 1, mid_mine, mid_other)
    gdot[...] = jnp.sum(grad * wg[...].reshape(2 * CH, D).astype(F32), axis=0, keepdims=True)
    cp("out", mid_other, mid_other_h)
    cp("out", mid_mine, mid_mine_h)
    cp("out", gdot, gdot_h)
    cp.finish()


def k_last(
    me, gat0, gat1, gat2, gat3, tab_h, perm_h, g_h, q_h, lam_h, nf_h, t_h, enter_h, pre_h, normed_h, gain_h, gdot_h, gpart_h, *rest
):
    pieces = rest[:8]
    bpi_h, bpf_h, small_h, mine_h, other_h = rest[8:13]
    (order, tab, perm, g, q, lam, nf, t, enter, pre, normed, gain, gdot, gpart, w, bpi, bpf, mine, other, lead, sums,
     small, sems) = rest[13:]
    cp = Copies(sems)
    summaries(cp, me, (gat0, gat1, gat2, gat3), order)
    cp("order", tab_h, tab)
    cp("order", perm_h, perm)
    cp("a", g_h, g)
    cp("a", q_h, q)
    cp("a", lam_h, lam)
    cp("a", nf_h, nf)
    cp("a", t_h, t)
    cp("a", enter_h, enter)
    cp("a", pre_h, pre)
    cp("b", normed_h, normed)
    cp("b", gain_h, gain)
    cp("b", gdot_h, gdot)
    cp("b", gpart_h, gpart)
    fetch_mix(cp, "b", pieces, (0, 3), w, 0)
    cp.wait("order")
    c512, s512 = row(tab, C512), row(tab, S512)
    c64, s64 = row(tab, C64), row(tab, S64)
    er = jnp.zeros((1, CH), F32)
    ei = jnp.zeros((1, CH), F32)
    for d in range(31, 0, -1):
        pd, sr, si = summary_of(order, me, d)
        nr = sr + pd * (c512 * er + s512 * ei)
        ni = si + pd * (c512 * ei - s512 * er)
        er = jnp.where(d > me[0], nr, er)
        ei = jnp.where(d > me[0], ni, ei)
    sums[...] = jnp.zeros_like(sums)
    sums[0:1, :] = er
    sums[1:2, :] = ei
    back = exact_t(sums[0:SEG, :], perm[...])
    er = back[0:1, :]
    ei = back[1:2, :]
    cp.wait("a")
    for b in range(SEG - 1, -1, -1):
        lead[b : b + 1, :] = er
        lead[SEG + b : SEG + b + 1, :] = ei
        a0 = row(lam, b) * wide(row(nf, b))
        tr = a0 * (g[b : b + 1, 0:CH] + row(q, b) * er)
        ti = a0 * (g[b : b + 1, CH:] + row(q, b) * ei)
        er = c64 * tr + s64 * ti
        ei = c64 * ti - s64 * tr
    sums[...] = jnp.zeros_like(sums)

    def chunk(r, i, sr, si):
        ber = lead[0:SEG, :]
        bei = lead[SEG : 2 * SEG, :]
        ber = jnp.concatenate([ber, ber], axis=0)
        bei = jnp.concatenate([bei, bei], axis=0)
        qq = q[r, :]
        gr = g[r, 0:CH] + qq * ber
        gi = g[r, CH:] + qq * bei
        ct, st = turns(tab, i, 2)
        l = lam[r, :]
        keep_carry = wide(nf[r, :])
        adm = 1.0 - l
        xr = pre[r, 0:CH]
        xi = pre[r, CH:]
        zr = jax.nn.sigmoid(xr)
        zi = jax.nn.sigmoid(xi)
        ur = gr * ct - gi * st
        ui = gr * st + gi * ct
        dot_s = gr * sr + gi * si
        turn = gi * sr - gr * si
        back_lam = keep_carry * dot_s - (ur * (xr * zr) + ui * (xi * zi))
        bf = back_lam * l * adm
        bpf[r, :] = bf.astype(BF16)
        bpi[r, 0:CH] = (adm * ur * (zr * (1.0 + xr * (1.0 - zr)))).astype(BF16)
        bpi[r, CH:] = (adm * ui * (zi * (1.0 + xi * (1.0 - zi)))).astype(BF16)
        rot = l * keep_carry * turn
        sums[0:SEG, :] += bf[0:SEG, :] + bf[SEG : 2 * SEG, :]
        sums[SEG : 2 * SEG, :] += rot[0:SEG, :] + rot[SEG : 2 * SEG, :]

    chunk(
        pl.ds(0, 2 * SEG),
        0,
        jnp.concatenate([enter[0:SEG, :], t[0:SEG, 0:CH]], axis=0),
        jnp.concatenate([enter[SEG : 2 * SEG, :], t[0:SEG, CH:]], axis=0),
    )

    def step(r, i):
        before = pl.ds(pl.multiple_of(i * 16 - SEG, SEG), 16)
        chunk(r, i, t[before, 0:CH], t[before, CH:])

    loop(ROWS // 16, 16, step, 1, 1)
    cp("out", bpi, bpi_h)
    cp("out", bpf, bpf_h)
    cp.wait("b")
    n = normed[...]
    grad = tn(bpi[...], n)
    put_grad(grad[:CH], 0, mine, other)
    put_grad(grad[CH:], 1, mine, other)
    dots = gdot[...] + jnp.sum(grad * w[0:2].reshape(2 * CH, D).astype(F32), axis=0, keepdims=True)
    grad = tn(bpf[...], n)
    put_grad(grad, 2, mine, other)
    dots = dots + jnp.sum(grad * w[2].astype(F32), axis=0, keepdims=True)
    cp("out", other, other_h)
    cp("out", mine, mine_h)
    first = me[0] % 2 == 0
    small[...] = jnp.zeros_like(small)
    for i, part in enumerate((dots / gain[...], gpart[...])):
        own, rest_half = part[:, :H], part[:, H:]
        small[2 * i : 2 * i + 1, :] = jnp.where(first, own, rest_half)
        small[2 * i + 1 : 2 * i + 2, :] = jnp.where(first, rest_half, own)
    total_b = jnp.sum(sums[0:SEG, :], axis=0, keepdims=True)
    total_r = jnp.sum(sums[SEG : 2 * SEG, :], axis=0, keepdims=True)
    sums[...] = jnp.zeros_like(sums)
    sums[0:1, :] = total_b
    sums[1:2, :] = total_r
    small[4:6, :] = exact(sums[0:SEG, :], perm[...])[0:2]
    cp("out", small, small_h)
    cp.finish()


def k_input(x_h, keep_h, gain_h, bm_h, bpi_h, bpf_h, bpg_h, *rest):
    pieces = rest[:8]
    grad_h, w, x, keep, gain, bm, bpi, bpf, bpg, bn, grad, sems = rest[8:]
    cp = Copies(sems)
    cp("a", bpi_h, bpi)
    fetch_mix(cp, "a", pieces, (0, 2), w, 0)
    cp("b", bpf_h, bpf)
    cp("b", bpg_h, bpg)
    fetch_mix(cp, "b", pieces, (2, 3), w, 2)
    cp("c", x_h, x)
    cp("c", keep_h, keep)
    cp("c", gain_h, gain)
    cp("c", bm_h, bm)
    cp.wait("a")
    bn[...] = nn(bpi[...], w[0:2].reshape(2 * CH, D))
    cp.wait("b")
    bn[...] += nn(bpf[...], w[2]) + nn(bpg[...], w[3:5].reshape(2 * CH, D))
    cp.wait("c")

    def norm(r, i):
        v = x[r, :].astype(F32)
        rs = lax.rsqrt(jnp.mean(v * v, axis=-1, keepdims=True) + EPS)
        u1 = bn[r, :] * gain[...] * keep[r, :1]
        m = jnp.mean(u1 * v, axis=-1, keepdims=True)
        grad[r, :] = (bm[r, :] + rs * u1 - v * (rs * rs * rs * m)).astype(BF16)

    loop(8, 64, norm)
    cp("out", grad, grad_h)
    cp.finish()


ANY = pl.BlockSpec(memory_space=pl.ANY)
SM = pl.BlockSpec(memory_space=pltpu.SMEM)


def call(kernel, args, outs, scratch, copies, scalar=True, vmem=60, us=5):
    specs = [ANY] * len(args)
    if scalar:
        specs[0] = SM
    return pl.pallas_call(
        kernel,
        in_specs=specs,
        out_specs=[ANY] * len(outs),
        out_shape=[jax.ShapeDtypeStruct(s, t) for s, t in outs],
        scratch_shapes=[pltpu.VMEM(s, t) for s, t in scratch] + [pltpu.SemaphoreType.DMA((copies,))],
        compiler_params=pltpu.CompilerParams(vmem_limit_bytes=vmem * 1024 * 1024),
        name=kernel.__name__,
        cost_estimate=pl.CostEstimate(flops=us, bytes_accessed=us, transcendentals=0),
    )(*args)


def device(z, y, c):
    return ((z % NZ) * NY + (y % NY)) * 2 + c


EVERY = [(z, y, c) for z in range(NZ) for y in range(NY) for c in range(2)]


def swap_core(v):
    return lax.ppermute(v, "ch", [(device(z, y, c), device(z, y, 1 - c)) for z, y, c in EVERY])


def move_z(v, k):
    return lax.ppermute(v, "ch", [(device(z, y, c), device(z + k, y, c)) for z, y, c in EVERY])


def move_y(v, k):
    return lax.ppermute(v, "ch", [(device(z, y, c), device(z, y + k, c)) for z, y, c in EVERY])


def move_x(v, k):
    return lax.ppermute(v, "dp", [(i, (i + k) % NX) for i in range(NX)])


def partner(i, c, k):
    return (i, i ^ 1, 3 - i, i ^ 2)[SWAP[k] if c else k]


def exchange_z(v, k):
    return lax.ppermute(v, "ch", [(device(z, y, c), device(partner(z, c, k), y, c)) for z, y, c in EVERY])


def exchange_y(v, k):
    return lax.ppermute(v, "ch", [(device(z, y, c), device(z, partner(y, c, k), c)) for z, y, c in EVERY])


def exchange_x(v, k):
    return lax.ppermute(
        v,
        ("dp", "ch"),
        [(x * 32 + device(z, y, c), partner(x, c, k) * 32 + device(z, y, c)) for x in range(NX) for z, y, c in EVERY],
    )


def after(value, *others):
    return lax.optimization_barrier((value,) + others)[0]


def gather_chip(mine, other, rows, core):
    got = swap_core(other)[:, :rows]
    mine = mine[:, :rows]
    return jnp.where(
        core == 0, jnp.concatenate([mine, got], axis=1), jnp.concatenate([got, mine], axis=1)
    )


def gather_line(v, move):
    return [v] + [move(v, -k) for k in (1, 2, 3)]


def gather_ring(v, exchange, earlier=None):
    one, two = exchange(v, 1), exchange(v, 2)
    if earlier is not None:
        one, two = lax.optimization_barrier((one, two) + earlier)[:2]
    return [v, one, two, exchange(one, 2)]


def summary_pair(summary):
    return summary[0] + swap_core(summary[1])


def summary_line(pair):
    line = gather_line(pair, move_z)
    return sum(jnp.pad(v, ((SEG * k, SEG * (3 - k)), (0, 0))) for k, v in enumerate(line))


def add4(own, near, far, near_too):
    a, b, c, d = [v.astype(F32) for v in (own, near, far, near_too)]
    return (a + c) + (b + d)


def reduce_core(mine, other):
    return (mine.astype(F32) + swap_core(other).astype(F32)).astype(BF16)


def reduce_pieces(pieces, move):
    return add4(pieces[0], *[move(pieces[k], k) for k in (1, 2, 3)])


def reduce_outer(pieces, exchange):
    return add4(pieces[0], *[exchange(pieces[k], k) for k in (1, 3, 2)])


def finish(keep, send, core):
    got = swap_core(send)
    return jnp.where(
        core == 0, jnp.concatenate([keep, got], axis=-1), jnp.concatenate([got, keep], axis=-1)
    )


def finish_units(own, core):
    keep = jnp.where(core == 0, own[:, :12], own[:, 12:])
    send = jnp.where(core == 0, own[:, 12:], own[:, :12])
    return finish(keep, send, core)


def finish_mlp(chip, core, xi):
    groups = gather_line(chip, move_x)

    def of_plane(g):
        k = (g + NX - xi) % NX
        return jnp.where(k < 2, jnp.where(k == 0, groups[0], groups[1]), jnp.where(k == 2, groups[2], groups[3]))

    kinds = jnp.stack([of_plane(g) for g in range(NX)]).reshape(3, 2, 48, H)
    keep = jnp.where(core == 0, kinds[:, 0], kinds[:, 1])
    send = jnp.where(core == 0, kinds[:, 1], kinds[:, 0])
    return finish(keep, send, core).astype(F32)


def halves(rows):
    hi = lax.reduce_precision(rows, 8, 7)
    return jnp.concatenate([hi, lax.reduce_precision(rows - hi, 8, 7)], axis=0).astype(BF16)


def end_phase(pieces, small, move, reduce):
    units, rows = pieces[0].shape[0], pieces[0].shape[0] * pieces[0].shape[1]
    tail = halves(small)
    total = reduce([jnp.concatenate([p.reshape(rows, H), tail], axis=0) for p in pieces], move)
    return total[:rows].astype(BF16).reshape(units, -1, H), total[rows : rows + 8] + total[rows + 8 :]


def to_steps(v):
    return v.reshape(SEG, STEPS, *v.shape[1:]).swapaxes(0, 1).reshape(v.shape)


def from_steps(v):
    return v.reshape(STEPS, SEG, *v.shape[1:]).swapaxes(0, 1).reshape(v.shape)


def shards(
    block_input, gain_mix, w_input, w_forget, w_outgate, bias_forget, rotation, w_out,
    gain_mlp, w_gate, w_up, w_down, seq_lengths, pad_mask, cotangent,
):
    place = lax.axis_index("ch").astype(jnp.int32)
    xi = lax.axis_index("dp").astype(jnp.int32)
    core = place % 2
    y = (place // 2) % NY
    z = place // (2 * NY)

    def own_first(v):
        return jnp.where(core == 0, v, jnp.concatenate([v[..., H:], v[..., :H]], axis=-1))

    vec = jnp.concatenate([bias_forget, rotation])
    hi = lax.reduce_precision(vec, 8, 7)
    mid = lax.reduce_precision(vec - hi, 8, 7)
    extra = jnp.concatenate([hi, mid, vec - hi - mid]).astype(BF16)
    me = jnp.stack([place, xi])
    mix_mine, mix_other, mlp_mine, mlp_other = call(
        k_pack,
        [me, w_input.T, w_forget.T, w_outgate.T, w_out, w_gate.T, w_up.T, w_down],
        [((MIX_U, 16, H), BF16)] * 2 + [((3, 48, H), BF16)] * 2,
        [((24, D), BF16), ((12, D), BF16), ((24, D), BF16), ((24, D), BF16), ((3, 48, D), BF16)]
        + [((MIX_U, 16, H), BF16)] * 2 + [((3, 48, H), BF16)] * 2,
        11,
    )
    rows = MIX_U * UNIT
    mix_chip = gather_chip(mix_mine, mix_other, 12, core).reshape(rows, H)
    mix_chip = jnp.concatenate([mix_chip, jnp.pad(extra[None], ((0, 7), (0, H - 72)))], axis=0)
    mlp_chip = gather_chip(mlp_mine, mlp_other, 48, core)
    mix_line = gather_line(mix_chip, move_y)
    mlp_line = gather_line(mlp_chip, move_z)
    mlp_line = jnp.concatenate(mlp_line, axis=1)
    mlp_line, place, gain_mix, gain_mlp, block_input, cotangent, seq_lengths, pad_mask = lax.optimization_barrier(
        (mlp_line, place, gain_mix, gain_mlp, block_input, cotangent, seq_lengths, pad_mask)
    )
    core = place % 2
    y = (place // 2) % NY
    z = place // (2 * NY)
    mix_line = jnp.concatenate(
        [jnp.concatenate([f[:rows].reshape(MIX_U, UNIT, H) for f in mix_line], axis=1).reshape(VEC, H)]
        + [f[rows:] for f in mix_line],
        axis=0,
    )
    j = jnp.arange(CH, dtype=jnp.int32)
    rest = j % 96
    ky, tail = rest // UNIT, rest % UNIT
    flip = jnp.where(core == 0, jnp.array([0, 1, 3, 2]), jnp.array([0, 3, 1, 2])).astype(jnp.int32)
    where_to = jnp.bitwise_xor(jnp.repeat(flip, 96), z) * 96 + ((ky + y) % NY) * UNIT + tail
    perm = (where_to[:, None] == j[None, :]).astype(F32)

    lengths = seq_lengths[0]
    ends = jnp.sum(jnp.where(jnp.arange(8)[:, None] >= jnp.arange(8)[None, :], lengths[None, :], 0), axis=1)
    starts = ends - lengths
    r = jnp.arange(ROWS, dtype=jnp.int32)
    position = place * ROWS + (r % SEG) * STEPS + r // SEG
    first = jnp.any(position[:, None] == starts[None, :], axis=1)
    nf = jnp.broadcast_to(1.0 - first.astype(F32)[:, None], (ROWS, 128))
    keep = jnp.broadcast_to(to_steps(pad_mask.astype(F32))[:, None], (ROWS, 128))

    x = own_first(to_steps(block_input))
    ups = own_first(to_steps(cotangent)) * keep[:, :1].astype(BF16)
    gain1 = own_first(gain_mix)[None]
    gain2 = own_first(gain_mlp)[None]
    wide_f = ((ROWS, D), F32)
    wide_b = ((ROWS, D), BF16)
    half_f = ((ROWS, CH), F32)
    half_b = ((ROWS, CH), BF16)
    lanes = ((ROWS, 128), F32)
    tab_s = ((TAB, CH), F32)
    perm_s = ((CH, CH), F32)
    few = ((SEG, CH), F32)
    pair = ((2 * SEG, CH), F32)
    gain_s = ((1, D), F32)
    order_s = ((16 * SEG, CH), F32)

    (normed,) = call(
        k_norm, [x, keep, gain1], [wide_b], [wide_b, lanes, gain_s, wide_b], 4, scalar=False, us=3
    )
    mix_swapped = swap_core(after(mix_line, mlp_line))
    mix_own = gather_ring(mix_line, exchange_z, (normed, ups, nf, perm, mix_swapped))
    mix_w = mix_own + [mix_swapped] + [swap_core(p) for p in mix_own[1:3]]
    mlp_own = gather_ring(mlp_line, exchange_y, (mix_own[3],))
    mix_w.append(swap_core(after(mix_own[3], *mix_w[4:], mlp_own[1], mlp_own[2])))
    mlp_early = lax.optimization_barrier((mlp_own[0], mlp_own[1]) + tuple(mix_w[4:]))[:2]
    mlp_early = [swap_core(p) for p in mlp_early]
    pre, s, lam, cum, tab, *summary = call(
        k_project,
        [me, normed, nf, perm] + mix_w,
        [wide_f, wide_f, half_f, half_f, tab_s, few, few],
        [((3, CH, D), BF16), wide_b, lanes, perm_s, ((256, H), BF16), wide_f, half_f, wide_f, half_f, half_f, tab_s,
         pair],
        44,
        us=6,
    )
    summary, mlp_early = lax.optimization_barrier((summary, mlp_early))
    line, mlp_own = lax.optimization_barrier((summary_line(summary_pair(summary)), mlp_own))
    before = gather_line(line, move_y)
    mlp_w = mlp_own + mlp_early + [swap_core(p) for p in mlp_own[2:]]
    hidden = ((ROWS, FF), BF16)
    mlp_g = ((4, 3, 4 * 96, H), BF16)
    mlp_s = ((12, 4 * 96, H), BF16)
    mid_g = ((4, 4, 96, H), BF16)
    t, enter, out, bm, g, q, bpg, gpart, gdot, *summary_back, mlp_mine, mlp_other, mid_mine, mid_other = call(
        k_middle,
        [me] + before + [tab, perm, s, cum, normed, x, gain2, ups, lam, nf] + mix_w + mlp_w,
        [wide_f, pair, wide_b, wide_f, wide_f, half_f, wide_b, gain_s, gain_s, few, few, mlp_g, mlp_g, mid_g, mid_g],
        [((2, CH, D), BF16), ((2, CH, D), BF16), ((3, FF, D), BF16), order_s, tab_s, perm_s, wide_f, half_f, wide_b,
         wide_b, gain_s, wide_b, half_f, lanes, pair, pair, wide_f, wide_b, wide_f, wide_b, hidden, hidden, hidden, mlp_s,
         mlp_s, wide_f, wide_b, wide_f, half_f, wide_b, gain_s, gain_s, mid_g, mid_g],
        150,
        vmem=62,
        us=20,
    )
    pair_back = summary_pair(summary_back)
    mlp_other, mid_other, pair_back = lax.optimization_barrier((mlp_other, mid_other, pair_back))
    mlp_swapped = swap_core(mlp_other)
    mlp_send = (mlp_mine[2:].astype(F32) + mlp_swapped[2:].astype(F32)).astype(BF16)
    line = after(summary_line(pair_back), mlp_send)
    mid_both = after(reduce_core(mid_mine, mid_other), line)
    behind = gather_line(line, move_y)
    mlp_got = exchange_x(mlp_send, 1)
    mid_slots = jnp.stack([mid_both[k] for k in SWAP])
    mid_got = exchange_z(mid_slots[2:], 1)
    behind[0] = after(behind[0], mid_got)
    end_g = ((4, 3, 96, H), BF16)
    bpi, bpf, small, end_mine, end_other = call(
        k_last,
        [me] + behind + [tab, perm, g, q, lam, nf, t, enter, pre, normed, gain1, gdot, gpart] + mix_w,
        [wide_b, half_b, few, end_g, end_g],
        [order_s, tab_s, perm_s, wide_f, half_f, half_f, lanes, wide_f, pair, wide_f, wide_b, gain_s, gain_s, gain_s,
         ((3, CH, D), BF16), wide_b, half_b, end_g, end_g, pair, pair, few],
        80,
        us=6,
    )
    mlp_two = mlp_mine[:2].astype(F32) + mlp_swapped[:2].astype(F32)
    mlp_two = (mlp_two.astype(BF16).astype(F32) + after(mlp_got, bpi).astype(F32)).astype(BF16)
    mid_two = (mid_slots[:2].astype(F32) + after(mid_got, bpi).astype(F32)).astype(BF16)
    small, mid_two = lax.optimization_barrier((small, mid_two))
    end_both = reduce_core(end_mine, end_other)
    small = small + swap_core(small)
    bpi, end_both, small, mlp_two = lax.optimization_barrier((bpi, end_both, small, mlp_two))
    (grad_input,) = call(
        k_input,
        [x, keep, gain1, bm, bpi, bpf, bpg] + mix_w,
        [wide_b],
        [((5, CH, D), BF16), wide_b, lanes, gain_s, wide_f, wide_b, half_b, wide_b, wide_f, wide_b],
        54,
        scalar=False,
        us=5,
    )
    mid_line = (mid_two[0].astype(F32) + after(exchange_z(mid_two[1], 2), grad_input).astype(F32)).astype(BF16)
    mlp_got = after(exchange_x(mlp_two[1], 2), grad_input)
    mlp_own = (mlp_two[0].astype(F32) + mlp_got.astype(F32)).astype(BF16)

    def z_phase(pieces):
        got = [exchange_z(pieces[k], k) for k in (1, 3, 2)]
        got = lax.optimization_barrier((*got, mlp_own))
        return add4(pieces[0], *got[:3])

    end_line, small = end_phase([end_both[k] for k in range(4)], small, None, lambda pieces, move: z_phase(pieces))
    end_line, mlp_own, grad_input, out = lax.optimization_barrier((end_line, mlp_own, grad_input, out))
    mlp_own = mlp_own.reshape(3, 4, 96, H)
    line = jnp.concatenate([end_line, mid_line], axis=0).reshape(MIX_U, 4, UNIT, H)
    own, small = end_phase([line[:, k] for k in range(4)], small, move_y, reduce_pieces)
    own = jnp.concatenate([own.reshape(MIX_U * UNIT, H), halves(small)], axis=0)
    mlp_slots = jnp.stack([mlp_own[:, k] for k in SWAP])
    mlp_two = (mlp_slots[:2].astype(F32) + exchange_y(mlp_slots[2:], 1).astype(F32)).astype(BF16)
    own, mlp_two = lax.optimization_barrier((own, mlp_two))
    mlp_line = mlp_two[0].astype(F32) + exchange_y(mlp_two[1], 2).astype(F32)
    mlp_line = mlp_line.astype(BF16).reshape(3, 4, UNIT, H)
    *got, mlp_line = lax.optimization_barrier((*[move_x(own, k) for k in (1, 2, 3)], mlp_line))
    total = add4(own, *got)
    grads_mix = finish_units(total[: MIX_U * UNIT].reshape(MIX_U, UNIT, H), core)
    small = total[MIX_U * UNIT : MIX_U * UNIT + 8] + total[MIX_U * UNIT + 8 :]

    mlp_chip = reduce_pieces([mlp_line[:, k] for k in range(4)], move_z).astype(BF16)
    grads_mlp = finish_mlp(mlp_chip, core, xi)
    bias_grad = lax.dynamic_slice(small[4], (place * 12,), (12,))
    rot_grad = lax.dynamic_slice(small[5], (place * 12,), (12,))

    def together(re_im):
        return re_im.swapaxes(0, 1).reshape(UNIT, D)

    return (
        from_steps(own_first(out)),
        from_steps(own_first(grad_input)),
        small[0:2].reshape(D),
        together(grads_mix[0:2]).T,
        grads_mix[2].T,
        together(grads_mix[3:5]).T,
        bias_grad,
        rot_grad,
        together(grads_mix[5:7]),
        small[2:4].reshape(D),
        grads_mlp[0].T,
        grads_mlp[1].T,
        grads_mlp[2],
    )


def solution(mesh):
    rows = P(("dp", "ch"), None)
    cols = P(None, "ch")
    return jax.shard_map(
        shards,
        mesh=mesh,
        in_specs=(
            rows, P(), cols, cols, cols, P("ch"), P("ch"), P("ch", None), P(), cols, cols,
            P("ch", None), P("dp", None), P(("dp", "ch")), rows,
        ),
        out_specs=(
            rows, rows, P(), cols, cols, cols, P("ch"), P("ch"), P("ch", None), P(), cols, cols,
            P("ch", None),
        ),
        check_vma=False,
    )
```
